768 devices in a mesh: dp: 128 (over y, x, z_hi, core), tensor: 6 (over z_lo).
Axes of the slice: x: 4, y: 8, z: 12 (z_hi: 2, z_lo: 6; z = z_hi * 6 + z_lo), core: 2. Of those that a mesh axis runs over, the one named last changes fastest.
Arguments:
- hidden: bfloat16 [49152, 3840], P('dp', 'tensor'), may hold values from -36 to 36
- targets: int32 [49152], P('dp'), may hold values from 0 to 31999
- padding: int32 [49152], P('dp'), may hold values 0 or 1
- gold_logit: float32 [49152], P('dp'), may hold values from 0 to 6
- vocab_lse: float32 [49152], P('dp'), may hold values from 6 to 10
- cotangent: float32 [49152], P('dp'), may hold values from -6 to 6
Outputs:
- grad_hidden: bfloat16 [49152, 3840], P('dp', 'tensor')
The draws below stay inside these ranges and needn't reach their ends.
All inputs are finite; a program needn't handle non-finite values. No bound on the sum of `padding` on one device may be relied on, other than what follows from the above.
Results may differ from the reference program's by a relative error of at most 0.0075.
Values may be sent and summed in bfloat16 or wider, within the bound.
No kernel may reach another device: no remote copies, remote signals or barrier semaphores. Data moves between devices by JAX's collectives and lax.ppermute only.
A program may use at most 32 MiB of HBM per device.

```python
import math
import jax
import jax.numpy as jnp
import numpy as np
from jax import lax

KW = 3840
TOK_DEV = 384
SPAN = 4
TOKENS = 49152
N_DP = 128


def draw_hidden(key, part):
    key = jax.random.fold_in(key, 5)
    base = jax.random.truncated_normal(key, -6.0, 6.0, (TOKENS, KW), jnp.float32)
    return base.astype(jnp.bfloat16)


def set_ends(entries, stream_key, least, largest):
    index_at = [jax.random.randint(jax.random.fold_in(stream_key, axis), (), 0, length) for axis, length in enumerate(entries.shape)]
    main_axis = entries.shape.index(max(entries.shape))
    next_to = index_at[:main_axis] + [(index_at[main_axis] + 1) % entries.shape[main_axis]] + index_at[main_axis + 1:]
    return entries.at[tuple(index_at)].set(least).at[tuple(next_to)].set(largest)


def block_scale(key, extent, split, low, high):
    def one(dim, shards_of):
        steps = jax.random.uniform(jax.random.fold_in(jax.random.fold_in(key, 6), dim), (shards_of,), jnp.float32, low / len(split), high / len(split))
        return jnp.repeat(jnp.exp(steps), extent[dim] // shards_of).reshape((-1,) + (1,) * (len(extent) - dim - 1))

    gain = one(*split[0])
    for cut in split[1:]:
        gain = gain * one(*cut)
    return gain


def rank_bounds(number_of, lean):
    loads = [(1 << 20) // math.isqrt(rank ** lean) + 1 for rank in range(1, number_of + 1)]
    deviation = 1 + sum(loads) // (1 << 30)
    return np.cumsum(np.array([max(1, weight // deviation) for weight in loads]))


def skewed_ids(stream_key, extent, amount, slope):
    listing = rank_bounds(amount, slope)
    ticket = jax.random.randint(jax.random.fold_in(stream_key, 1), extent, 0, int(listing[amount - 1]))
    standing = jnp.searchsorted(jnp.asarray(listing, jnp.int32), ticket, side="right")
    return jax.random.permutation(jax.random.fold_in(stream_key, 2), amount)[standing].astype(jnp.int32)


def noise(key, extent, scale, limit, cuts=(), held_as=jnp.bfloat16):
    array = scale * jax.random.normal(key, extent, jnp.float32)
    if cuts:
        array = array * block_scale(key, extent, cuts, -0.22, 0.18)
    return jnp.clip(array, -limit, limit).astype(held_as)


def setup_inputs(seed: int = 0) -> dict:
    key_list = jax.random.split(jax.random.key(seed), 7)
    return {
        "hidden": draw_hidden(jax.random.fold_in(key_list[6], 71), 0),
        "targets": set_ends(skewed_ids(key_list[1], (TOKENS,), 32000, 2), jax.random.fold_in(key_list[1], 3), 0, 31999).astype(jnp.int32),
        "padding": set_ends((jax.random.randint(key_list[2], (TOKENS,), 0, 8) < 7).astype(jnp.int32), jax.random.fold_in(key_list[2], 1), 0, 1),
        "gold_logit": jnp.clip(6.0 * jax.random.uniform(key_list[3], (TOKENS,), jnp.float32) ** block_scale(key_list[3], (TOKENS,), ((0, 128),), -0.2, 0.2), 0.0, 6.0),
        "vocab_lse": jnp.clip(6.0 + 4.0 * jax.random.uniform(key_list[4], (TOKENS,), jnp.float32) ** block_scale(key_list[4], (TOKENS,), ((0, 128),), -0.2, 0.2), 6.0, 10.0),
        "cotangent": noise(key_list[5], (TOKENS,), 1.0, 6.0, ((0, 128),), jnp.float32),
    }


def normalizer(scores, allowed, outside):
    masked = jnp.where(allowed, scores, -1e+30)
    peak_value = jnp.maximum(outside, lax.optimization_barrier(jnp.max(masked, axis=(1, 2))))
    denominator = jnp.exp(outside - peak_value) + lax.optimization_barrier(jnp.sum(jnp.where(allowed, jnp.exp(scores - peak_value[:, None, None]), 0.0), axis=(1, 2)))
    return peak_value + jnp.log(denominator)

def slope_tile(scores, usable, matches, total_lse, pos_lse, weight, score_scale):
    spread = jnp.where(usable, jnp.exp(scores - total_lse), 0.0) - jnp.where(matches, jnp.exp(scores - pos_lse), 0.0)
    return (weight * spread * score_scale).astype(jnp.bfloat16)

def reference(hidden, targets, padding, gold_logit, vocab_lse, cotangent):
    score_scale = 1.0 / math.sqrt(KW)
    blocks = hidden.reshape(N_DP, TOK_DEV, KW)
    label_code = jnp.where(padding == 1, targets, -1).reshape(N_DP, TOK_DEV)
    target_rows = targets.reshape(N_DP, TOK_DEV)
    weight_rows = (cotangent * padding.astype(jnp.float32)).reshape(N_DP, TOK_DEV)
    gold_rows = gold_logit.reshape(N_DP, TOK_DEV)
    vocab_rows = vocab_lse.reshape(N_DP, TOK_DEV)
    offsets = jnp.arange(1, SPAN + 1, dtype=jnp.int32)

    def forward_block(block_index):
        window = ((block_index - offsets) % N_DP).astype(jnp.int32)
        keys_window = jnp.take(blocks, window, axis=0)
        key_labels = jnp.take(label_code, window, axis=0)
        queries = jnp.take(blocks, block_index, axis=0)
        scores = jnp.einsum('tc,sjc->tsj', queries.astype(jnp.float32), keys_window.astype(jnp.float32)) * score_scale
        usable = (key_labels >= 0)[None]
        query_targets = jnp.take(target_rows, block_index, axis=0)
        matches = usable & (key_labels[None] == query_targets[:, None, None])
        total_lse = normalizer(scores, usable, jnp.take(vocab_rows, block_index, axis=0))
        pos_lse = normalizer(scores, matches, jnp.take(gold_rows, block_index, axis=0))
        weight = jnp.take(weight_rows, block_index, axis=0)
        return slope_tile(scores, usable, matches, total_lse[:, None, None], pos_lse[:, None, None], weight[:, None, None], score_scale)
    slopes_all = lax.map(forward_block, jnp.arange(N_DP, dtype=jnp.int32))

    def backward_block(block_index):
        window = ((block_index - offsets) % N_DP).astype(jnp.int32)
        keys_window = jnp.take(blocks, window, axis=0)
        own_slopes = jnp.take(slopes_all, block_index, axis=0)
        query_grad = jnp.einsum('tsj,sjc->tc', own_slopes.astype(jnp.float32), keys_window.astype(jnp.float32))
        later = ((block_index + offsets) % N_DP).astype(jnp.int32)
        gathered_slopes = jnp.take(slopes_all, later, axis=0)
        steps_range = jnp.arange(SPAN, dtype=jnp.int32)
        diagonal_tiles = gathered_slopes[steps_range, :, steps_range, :]
        query_rows = jnp.take(blocks, later, axis=0)
        key_grad = jnp.einsum('stj,stc->jc', diagonal_tiles.astype(jnp.float32), query_rows.astype(jnp.float32))
        return (query_grad + key_grad).astype(jnp.bfloat16)
    result = lax.map(backward_block, jnp.arange(N_DP, dtype=jnp.int32))
    return result.reshape(TOKENS, KW)
```

```python
import math

import jax
import jax.numpy as jnp
from jax import lax
from jax.sharding import PartitionSpec as P

KW = 3840
SEG = 384
BF = jnp.bfloat16
F32 = jnp.float32


def dp_shift(value, steps):
    count = lax.axis_size("dp")
    return lax.ppermute(value, "dp", [(i, (i + steps) % count) for i in range(count)])


def core_swap(value):
    count = lax.axis_size("dp")
    return lax.ppermute(value, "dp", [(i, i ^ 1) for i in range(count)])


def triple_shift(value, steps):
    pairs = [(3 * u + v, 3 * u + (v + steps) % 3) for u in range(2) for v in range(3)]
    return lax.ppermute(value, "tensor", pairs)


def triple_swap(value):
    return lax.ppermute(value, "tensor", [(r, (r + 3) % 6) for r in range(6)])


def rows_of(value, start, size):
    return lax.dynamic_slice_in_dim(value, start, size, 0)


def partial_of(queries, keys):
    return lax.dot_general(queries, keys, (((1,), (1,)), ((), ())), preferred_element_type=F32)


def reduced(hidden, keys, u, v):
    def group(steps):
        return partial_of(rows_of(hidden, ((v + steps) % 3) * 128, 128), keys)

    first = triple_shift(group(1), 1)
    second = triple_shift(group(2), 2)
    total = group(0) + first + second
    other = triple_swap(rows_of(total, (1 - u) * 64, 64))
    return rows_of(total, u * 64, 64) + other


def normalizer(parts, outside):
    peak = outside
    for scores, allowed in parts:
        peak = jnp.maximum(peak, jnp.max(jnp.where(allowed, scores, -1e30), axis=1))
    total = jnp.exp(outside - peak)
    for scores, allowed in parts:
        total = total + jnp.sum(jnp.where(allowed, jnp.exp(scores - peak[:, None]), 0.0), axis=1)
    return peak + jnp.log(total)


def gathered(mine, u, v):
    other = triple_swap(mine)
    low = jnp.where(u == 0, mine, other)
    high = jnp.where(u == 0, other, mine)
    group = jnp.concatenate([low, high], axis=0)
    first = triple_shift(group, 1)
    second = triple_shift(group, 2)
    full = jnp.zeros((SEG, mine.shape[1]), BF)
    full = lax.dynamic_update_slice_in_dim(full, group, v * 128, 0)
    full = lax.dynamic_update_slice_in_dim(full, first, ((v + 2) % 3) * 128, 0)
    return lax.dynamic_update_slice_in_dim(full, second, ((v + 1) % 3) * 128, 0)


def key_grad(slopes, hidden):
    return lax.dot_general(slopes, hidden, (((0,), (0,)), ((), ())), preferred_element_type=F32)


def per_device(hidden, targets, padding, gold_logit, vocab_lse, cotangent):
    score_scale = 1.0 / math.sqrt(KW)
    core = lax.axis_index("dp") % 2
    r = lax.axis_index("tensor")
    u, v = r // 3, r % 3
    label_code = jnp.where(padding == 1, targets, -1)
    weight = cotangent * padding.astype(F32)

    far = dp_shift(hidden, 2)
    near = dp_shift(hidden, 4)
    far_label = dp_shift(label_code, 2)
    near_label = dp_shift(label_code, 4)
    near_pair = core_swap(jnp.where(core == 0, hidden, near))
    far_pair = core_swap(far)
    pair_labels = core_swap(jnp.stack([jnp.where(core == 0, label_code, near_label), far_label]))

    near_keys = jnp.concatenate([near, near_pair], axis=0)
    far_keys = jnp.concatenate([far, far_pair], axis=0)
    near_labels = jnp.concatenate([near_label, pair_labels[0]])
    far_labels = jnp.concatenate([far_label, pair_labels[1]])

    near_scores = reduced(hidden, near_keys, u, v) * score_scale
    far_scores = reduced(hidden, far_keys, u, v) * score_scale

    base = v * 128 + u * 64
    row_targets = rows_of(targets, base, 64)
    parts = []
    for scores, labels in ((near_scores, near_labels), (far_scores, far_labels)):
        usable = jnp.broadcast_to((labels >= 0)[None], scores.shape)
        matches = usable & (labels[None] == row_targets[:, None])
        parts.append((scores, usable, matches))
    total_lse = normalizer([(s, a) for s, a, m in parts], rows_of(vocab_lse, base, 64))
    pos_lse = normalizer([(s, m) for s, a, m in parts], rows_of(gold_logit, base, 64))
    row_weight = rows_of(weight, base, 64)
    slopes = []
    for scores, usable, matches in parts:
        spread = jnp.where(usable, jnp.exp(scores - total_lse[:, None]), 0.0) - jnp.where(
            matches, jnp.exp(scores - pos_lse[:, None]), 0.0
        )
        slopes.append((row_weight[:, None] * spread * score_scale).astype(BF))
    full = gathered(jnp.concatenate(slopes, axis=1), u, v)

    far_back = core_swap(key_grad(full[:, 3 * SEG :], hidden).astype(BF))
    far_sum = key_grad(full[:, 2 * SEG : 3 * SEG], hidden) + far_back.astype(F32)
    far_home = dp_shift(far_sum.astype(BF), -2)
    near_back = core_swap(key_grad(full[:, SEG : 2 * SEG], hidden).astype(BF)).astype(F32)
    near_sum = key_grad(full[:, :SEG], hidden) + jnp.where(core == 1, near_back, 0.0)
    near_home = dp_shift(near_sum.astype(BF), -4)
    query_grad = jnp.dot(full[:, : 2 * SEG], near_keys, preferred_element_type=F32)
    query_grad = query_grad + jnp.dot(full[:, 2 * SEG :], far_keys, preferred_element_type=F32)
    query_grad = query_grad + jnp.where(core == 0, near_back, 0.0)
    return (query_grad + near_home.astype(F32) + far_home.astype(F32)).astype(BF)


def solution(mesh):
    placed = (P("dp", "tensor"), P("dp"), P("dp"), P("dp"), P("dp"), P("dp"))
    return jax.shard_map(
        per_device, mesh=mesh, in_specs=placed, out_specs=P("dp", "tensor"), check_vma=False
    )
```

```python
import math

import jax
import jax.numpy as jnp
from jax import lax
from jax.sharding import PartitionSpec as P

KW = 3840
SEG = 384
BF = jnp.bfloat16
F32 = jnp.float32


def dp_shift(value, steps):
    count = lax.axis_size("dp")
    return lax.ppermute(value, "dp", [(i, (i + steps) % count) for i in range(count)])


def core_swap(value):
    count = lax.axis_size("dp")
    return lax.ppermute(value, "dp", [(i, i ^ 1) for i in range(count)])


def odd_keys(value):
    count = lax.axis_size("dp")
    return lax.ppermute(value, "dp", [(i, (i + (1 if i % 2 == 0 else 3)) % count) for i in range(count)])


def odd_home(value):
    count = lax.axis_size("dp")
    return lax.ppermute(value, "dp", [((i + (1 if i % 2 == 0 else 3)) % count, i) for i in range(count)])


def triple_shift(value, steps):
    pairs = [(3 * u + v, 3 * u + (v + steps) % 3) for u in range(2) for v in range(3)]
    return lax.ppermute(value, "tensor", pairs)


def triple_swap(value):
    return lax.ppermute(value, "tensor", [(r, (r + 3) % 6) for r in range(6)])


def rows_of(value, start, size):
    return lax.dynamic_slice_in_dim(value, start, size, 0)


def partial_of(queries, keys):
    return lax.dot_general(queries, keys, (((1,), (1,)), ((), ())), preferred_element_type=F32)


def after(value, *others):
    return lax.optimization_barrier((value,) + others)[0]


def outgoing(hidden, keys, v):
    return tuple(
        partial_of(rows_of(hidden, ((v + steps) % 3) * 128, 128), keys) for steps in (1, 2)
    )


def normalizer(parts, outside):
    peak = outside
    for scores, allowed in parts:
        peak = jnp.maximum(peak, jnp.max(jnp.where(allowed, scores, -1e30), axis=1))
    total = jnp.exp(outside - peak)
    for scores, allowed in parts:
        total = total + jnp.sum(jnp.where(allowed, jnp.exp(scores - peak[:, None]), 0.0), axis=1)
    return peak + jnp.log(total)


def row_group(mine, other, u):
    low = jnp.where(u == 0, mine, other)
    high = jnp.where(u == 0, other, mine)
    return jnp.concatenate([low, high], axis=0)


def all_rows(group, first, second, v):
    full = jnp.zeros((SEG, group.shape[1]), BF)
    full = lax.dynamic_update_slice_in_dim(full, group, v * 128, 0)
    full = lax.dynamic_update_slice_in_dim(full, first, ((v + 2) % 3) * 128, 0)
    return lax.dynamic_update_slice_in_dim(full, second, ((v + 1) % 3) * 128, 0)


def key_grad(slopes, hidden):
    return lax.dot_general(slopes, hidden, (((0,), (0,)), ((), ())), preferred_element_type=F32)


def per_device(hidden, targets, padding, gold_logit, vocab_lse, cotangent):
    score_scale = 1.0 / math.sqrt(KW)
    core = lax.axis_index("dp") % 2
    r = lax.axis_index("tensor")
    u, v = r // 3, r % 3
    label_code = jnp.where(padding == 1, targets, -1)
    weight = cotangent * padding.astype(F32)

    far = dp_shift(hidden, 2)
    near = dp_shift(hidden, 4)
    odd = odd_keys(hidden)
    late_code = after(label_code, near)
    far_label = dp_shift(late_code, 2)
    near_labels = jnp.concatenate([dp_shift(late_code, 4), odd_keys(late_code)])
    far_labels = jnp.concatenate([far_label, core_swap(far_label)])
    own_rows = rows_of(hidden, v * 128, 128)

    near_keys = jnp.concatenate([near, odd], axis=0)
    near_out = outgoing(hidden, near_keys, v)
    near_group = partial_of(own_rows, near_keys)
    near_group = near_group + triple_shift(near_out[0], 1) + triple_shift(near_out[1], 2)
    near_send = rows_of(near_group, (1 - u) * 64, 64)
    near_other = triple_swap(near_send)

    far_keys = jnp.concatenate([far, core_swap(far)], axis=0)
    far_out = outgoing(hidden, far_keys, v)
    far_out = lax.optimization_barrier(far_out + (near_send,))
    far_group = partial_of(own_rows, far_keys)
    far_group = far_group + triple_shift(far_out[0], 1) + triple_shift(far_out[1], 2)
    far_other = triple_swap(rows_of(far_group, (1 - u) * 64, 64))
    near_scores = (rows_of(near_group, u * 64, 64) + near_other) * score_scale
    far_scores = (rows_of(far_group, u * 64, 64) + far_other) * score_scale

    base = v * 128 + u * 64
    row_targets = rows_of(targets, base, 64)
    parts = []
    for scores, labels in ((near_scores, near_labels), (far_scores, far_labels)):
        usable = jnp.broadcast_to((labels >= 0)[None], scores.shape)
        matches = usable & (labels[None] == row_targets[:, None])
        parts.append((scores, usable, matches))
    total_lse = normalizer([(s, a) for s, a, m in parts], rows_of(vocab_lse, base, 64))
    pos_lse = normalizer([(s, m) for s, a, m in parts], rows_of(gold_logit, base, 64))
    row_weight = rows_of(weight, base, 64)
    slopes = []
    for scores, usable, matches in parts:
        spread = jnp.where(usable, jnp.exp(scores - total_lse[:, None]), 0.0) - jnp.where(
            matches, jnp.exp(scores - pos_lse[:, None]), 0.0
        )
        slopes.append((row_weight[:, None] * spread * score_scale).astype(BF))
    near_mine, far_mine = slopes
    far_rows = row_group(far_mine, triple_swap(far_mine), u)
    near_other_rows = triple_swap(near_mine)
    far_one = triple_shift(far_rows, 1)
    far_two = triple_shift(far_rows, 2)
    near_rows = row_group(near_mine, after(near_other_rows, far_rows), u)
    near_one = triple_shift(near_rows, 1)
    near_two = triple_shift(near_rows, 2)

    far_full = all_rows(far_rows, far_one, far_two, v)
    far_back = core_swap(key_grad(far_full[:, SEG:], hidden).astype(BF))
    far_sum = key_grad(far_full[:, :SEG], hidden) + far_back.astype(F32)
    far_sum = far_sum.astype(BF)
    far_home = dp_shift(far_sum, -2)

    near_full = all_rows(near_rows, after(near_one, far_sum), near_two, v)
    near_home = dp_shift(key_grad(near_full[:, :SEG], hidden).astype(BF), -4)
    odd_back = odd_home(key_grad(near_full[:, SEG:], hidden).astype(BF))
    query_grad = jnp.dot(near_full, near_keys, preferred_element_type=F32)
    query_grad = query_grad + jnp.dot(far_full, far_keys, preferred_element_type=F32)
    home = near_home.astype(F32) + odd_back.astype(F32) + far_home.astype(F32)
    return (query_grad + home).astype(BF)


def solution(mesh):
    placed = (P("dp", "tensor"), P("dp"), P("dp"), P("dp"), P("dp"), P("dp"))
    return jax.shard_map(
        per_device, mesh=mesh, in_specs=placed, out_specs=P("dp", "tensor"), check_vma=False
    )
```

```python
import math

import jax
import jax.numpy as jnp
from jax import lax
from jax.sharding import PartitionSpec as P

KW = 3840
SEG = 384
BF = jnp.bfloat16
F32 = jnp.float32


def dp_shift(value, steps):
    count = lax.axis_size("dp")
    return lax.ppermute(value, "dp", [(i, (i + steps) % count) for i in range(count)])


def core_swap(value):
    count = lax.axis_size("dp")
    return lax.ppermute(value, "dp", [(i, i ^ 1) for i in range(count)])


def odd_keys(value):
    count = lax.axis_size("dp")
    return lax.ppermute(value, "dp", [(i, (i + (1 if i % 2 == 0 else 3)) % count) for i in range(count)])


def odd_home(value):
    count = lax.axis_size("dp")
    return lax.ppermute(value, "dp", [((i + (1 if i % 2 == 0 else 3)) % count, i) for i in range(count)])


def triple_shift(value, steps):
    pairs = [(3 * u + v, 3 * u + (v + steps) % 3) for u in range(2) for v in range(3)]
    return lax.ppermute(value, "tensor", pairs)


def triple_swap(value):
    return lax.ppermute(value, "tensor", [(r, (r + 3) % 6) for r in range(6)])


def rows_of(value, start, size):
    return lax.dynamic_slice_in_dim(value, start, size, 0)


def partial_of(queries, keys):
    return lax.dot_general(queries, keys, (((1,), (1,)), ((), ())), preferred_element_type=F32)


def with_codes(hidden, targets, padding):
    code = jnp.where(padding == 1, targets + 1, 0)
    digits = jnp.stack([code >> 8, code & 255]).astype(BF)
    tail = jnp.pad(digits, ((0, 14), (0, hidden.shape[1] - SEG)))
    return jnp.concatenate([hidden, tail], axis=0)


def codes_of(payload):
    digits = lax.optimization_barrier(payload[SEG:])[:2, :SEG].astype(F32)
    return digits[0] * 256.0 + digits[1]


def after(value, *others):
    return lax.optimization_barrier((value,) + others)[0]


def outgoing(hidden, keys, v):
    return tuple(
        partial_of(rows_of(hidden, ((v + steps) % 3) * 128, 128), keys) for steps in (1, 2)
    )


def normalizer(parts, outside):
    peak = outside
    for scores, allowed in parts:
        peak = jnp.maximum(peak, jnp.max(jnp.where(allowed, scores, -1e30), axis=1))
    total = jnp.exp(outside - peak)
    for scores, allowed in parts:
        total = total + jnp.sum(jnp.where(allowed, jnp.exp(scores - peak[:, None]), 0.0), axis=1)
    return peak + jnp.log(total)


def row_group(mine, other, u):
    low = jnp.where(u == 0, mine, other)
    high = jnp.where(u == 0, other, mine)
    return jnp.concatenate([low, high], axis=0)


def all_rows(group, first, second, v):
    full = jnp.zeros((SEG, group.shape[1]), BF)
    full = lax.dynamic_update_slice_in_dim(full, group, v * 128, 0)
    full = lax.dynamic_update_slice_in_dim(full, first, ((v + 2) % 3) * 128, 0)
    return lax.dynamic_update_slice_in_dim(full, second, ((v + 1) % 3) * 128, 0)


def key_grad(slopes, hidden):
    return lax.dot_general(slopes, hidden, (((0,), (0,)), ((), ())), preferred_element_type=F32)


def per_device(hidden, targets, padding, gold_logit, vocab_lse, cotangent):
    score_scale = 1.0 / math.sqrt(KW)
    core = lax.axis_index("dp") % 2
    r = lax.axis_index("tensor")
    u, v = r // 3, r % 3
    weight = cotangent * padding.astype(F32)
    payload = with_codes(hidden, targets, padding)

    far = dp_shift(payload, 2)
    near = dp_shift(payload, 4)
    odd = odd_keys(payload)
    own_rows = rows_of(hidden, v * 128, 128)

    near_keys = jnp.concatenate([near[:SEG], odd[:SEG]], axis=0)
    near_codes = jnp.concatenate([codes_of(near), codes_of(odd)])
    near_out = outgoing(hidden, near_keys, v)
    near_group = partial_of(own_rows, near_keys)
    near_group = near_group + triple_shift(near_out[0], 1) + triple_shift(near_out[1], 2)
    near_send = rows_of(near_group, (1 - u) * 64, 64)
    near_other = triple_swap(near_send)

    far_pair = core_swap(far)
    far_keys = jnp.concatenate([far[:SEG], far_pair[:SEG]], axis=0)
    far_codes = jnp.concatenate([codes_of(far), codes_of(far_pair)])
    far_out = outgoing(hidden, far_keys, v)
    far_out = lax.optimization_barrier(far_out + (near_send,))
    far_group = partial_of(own_rows, far_keys)
    far_group = far_group + triple_shift(far_out[0], 1) + triple_shift(far_out[1], 2)
    far_other = triple_swap(rows_of(far_group, (1 - u) * 64, 64))
    near_scores = (rows_of(near_group, u * 64, 64) + near_other) * score_scale
    far_scores = (rows_of(far_group, u * 64, 64) + far_other) * score_scale

    base = v * 128 + u * 64
    row_codes = rows_of(targets, base, 64).astype(F32) + 1.0
    parts = []
    for scores, codes in ((near_scores, near_codes), (far_scores, far_codes)):
        usable = jnp.broadcast_to((codes > 0.0)[None], scores.shape)
        matches = usable & (codes[None] == row_codes[:, None])
        parts.append((scores, usable, matches))
    total_lse = normalizer([(s, a) for s, a, m in parts], rows_of(vocab_lse, base, 64))
    pos_lse = normalizer([(s, m) for s, a, m in parts], rows_of(gold_logit, base, 64))
    row_weight = rows_of(weight, base, 64)
    slopes = []
    for scores, usable, matches in parts:
        spread = jnp.where(usable, jnp.exp(scores - total_lse[:, None]), 0.0) - jnp.where(
            matches, jnp.exp(scores - pos_lse[:, None]), 0.0
        )
        slopes.append((row_weight[:, None] * spread * score_scale).astype(BF))
    near_mine, far_mine = slopes
    far_rows = row_group(far_mine, triple_swap(far_mine), u)
    near_rows = row_group(near_mine, triple_swap(near_mine), u)
    far_rows, near_rows = lax.optimization_barrier((far_rows, near_rows))
    far_one = triple_shift(far_rows, 1)
    far_two = triple_shift(far_rows, 2)
    near_one = triple_shift(near_rows, 1)
    near_two = triple_shift(near_rows, 2)

    far_full = all_rows(far_rows, far_one, far_two, v)
    far_back = core_swap(key_grad(far_full[:, SEG:], hidden).astype(BF))
    far_sum = key_grad(far_full[:, :SEG], hidden) + far_back.astype(F32)
    far_sum = far_sum.astype(BF)
    far_home = dp_shift(far_sum, -2)

    near_full = all_rows(near_rows, after(near_one, far_sum), near_two, v)
    near_home = dp_shift(key_grad(near_full[:, :SEG], hidden).astype(BF), -4)
    odd_back = odd_home(key_grad(near_full[:, SEG:], hidden).astype(BF))
    query_grad = jnp.dot(near_full, near_keys, preferred_element_type=F32)
    query_grad = query_grad + jnp.dot(far_full, far_keys, preferred_element_type=F32)
    home = near_home.astype(F32) + odd_back.astype(F32) + far_home.astype(F32)
    return (query_grad + home).astype(BF)


def solution(mesh):
    placed = (P("dp", "tensor"), P("dp"), P("dp"), P("dp"), P("dp"), P("dp"))
    return jax.shard_map(
        per_device, mesh=mesh, in_specs=placed, out_specs=P("dp", "tensor"), check_vma=False
    )
```

```python
import math

import jax
import jax.numpy as jnp
from jax import lax
from jax.sharding import PartitionSpec as P

KW = 3840
SEG = 384
BF = jnp.bfloat16
F32 = jnp.float32


def dp_shift(value, steps):
    count = lax.axis_size("dp")
    return lax.ppermute(value, "dp", [(i, (i + steps) % count) for i in range(count)])


def core_swap(value):
    count = lax.axis_size("dp")
    return lax.ppermute(value, "dp", [(i, i ^ 1) for i in range(count)])


def odd_keys(value):
    count = lax.axis_size("dp")
    return lax.ppermute(value, "dp", [(i, (i + (1 if i % 2 == 0 else 3)) % count) for i in range(count)])


def odd_home(value):
    count = lax.axis_size("dp")
    return lax.ppermute(value, "dp", [((i + (1 if i % 2 == 0 else 3)) % count, i) for i in range(count)])


def triple_shift(value, steps):
    pairs = [(3 * u + v, 3 * u + (v + steps) % 3) for u in range(2) for v in range(3)]
    return lax.ppermute(value, "tensor", pairs)


def triple_swap(value):
    return lax.ppermute(value, "tensor", [(r, (r + 3) % 6) for r in range(6)])


def rows_of(value, start, size):
    return lax.dynamic_slice_in_dim(value, start, size, 0)


def partial_of(queries, keys):
    return lax.dot_general(queries, keys, (((1,), (1,)), ((), ())), preferred_element_type=F32)


def with_codes(hidden, targets, padding):
    code = jnp.where(padding == 1, targets + 1, 0)
    digits = jnp.stack([code >> 8, code & 255]).astype(BF)
    tail = jnp.pad(digits, ((0, 14), (0, hidden.shape[1] - SEG)))
    return jnp.concatenate([hidden, tail], axis=0)


def codes_of(payload):
    digits = lax.optimization_barrier(payload[SEG:])[:2, :SEG].astype(F32)
    return digits[0] * 256.0 + digits[1]


def after(value, *others):
    return lax.optimization_barrier((value,) + others)[0]


def outgoing(hidden, keys, v):
    return tuple(
        partial_of(rows_of(hidden, ((v + steps) % 3) * 128, 128), keys) for steps in (1, 2)
    )


def normalizer(parts, outside):
    peak = outside
    for scores, allowed in parts:
        peak = jnp.maximum(peak, jnp.max(jnp.where(allowed, scores, -1e30), axis=1))
    total = jnp.exp(outside - peak)
    for scores, allowed in parts:
        total = total + jnp.sum(jnp.where(allowed, jnp.exp(scores - peak[:, None]), 0.0), axis=1)
    return peak + jnp.log(total)


def row_group(mine, other, u):
    low = jnp.where(u == 0, mine, other)
    high = jnp.where(u == 0, other, mine)
    return jnp.concatenate([low, high], axis=0)


def all_rows(group, first, second, v):
    full = jnp.zeros((SEG, group.shape[1]), BF)
    full = lax.dynamic_update_slice_in_dim(full, group, v * 128, 0)
    full = lax.dynamic_update_slice_in_dim(full, first, ((v + 2) % 3) * 128, 0)
    return lax.dynamic_update_slice_in_dim(full, second, ((v + 1) % 3) * 128, 0)


def key_grad(slopes, hidden):
    return lax.dot_general(slopes, hidden, (((0,), (0,)), ((), ())), preferred_element_type=F32)


def per_device(hidden, targets, padding, gold_logit, vocab_lse, cotangent):
    score_scale = 1.0 / math.sqrt(KW)
    core = lax.axis_index("dp") % 2
    r = lax.axis_index("tensor")
    u, v = r // 3, r % 3
    weight = cotangent * padding.astype(F32)
    payload = with_codes(hidden, targets, padding)

    far = dp_shift(payload, 2)
    near = dp_shift(payload, 4)
    odd = odd_keys(payload)
    own_rows = rows_of(hidden, v * 128, 128)

    near_keys = jnp.concatenate([near[:SEG], odd[:SEG]], axis=0)
    near_codes = jnp.concatenate([codes_of(near), codes_of(odd)])
    near_out = outgoing(hidden, near_keys, v)
    near_out = lax.optimization_barrier(near_out + (far,))[:2]
    near_group = partial_of(own_rows, near_keys)
    near_in = (triple_shift(near_out[0], 1), triple_shift(near_out[1], 2))

    far_pair = core_swap(far)
    far_keys = jnp.concatenate([far[:SEG], far_pair[:SEG]], axis=0)
    far_codes = jnp.concatenate([codes_of(far), codes_of(far_pair)])
    far_out = outgoing(hidden, far_keys, v)
    near_group = near_group + after(near_in[0], *far_out) + near_in[1]
    near_other = triple_swap(rows_of(near_group, (1 - u) * 64, 64))
    far_group = partial_of(own_rows, far_keys)
    far_group = far_group + triple_shift(far_out[0], 1) + triple_shift(far_out[1], 2)
    far_other = triple_swap(rows_of(far_group, (1 - u) * 64, 64))
    near_scores = (rows_of(near_group, u * 64, 64) + near_other) * score_scale
    far_scores = (rows_of(far_group, u * 64, 64) + far_other) * score_scale

    base = v * 128 + u * 64
    row_codes = rows_of(targets, base, 64).astype(F32) + 1.0
    parts = []
    for scores, codes in ((near_scores, near_codes), (far_scores, far_codes)):
        usable = jnp.broadcast_to((codes > 0.0)[None], scores.shape)
        matches = usable & (codes[None] == row_codes[:, None])
        parts.append((scores, usable, matches))
    total_lse = normalizer([(s, a) for s, a, m in parts], rows_of(vocab_lse, base, 64))
    pos_lse = normalizer([(s, m) for s, a, m in parts], rows_of(gold_logit, base, 64))
    row_weight = rows_of(weight, base, 64)
    slopes = []
    for scores, usable, matches in parts:
        spread = jnp.where(usable, jnp.exp(scores - total_lse[:, None]), 0.0) - jnp.where(
            matches, jnp.exp(scores - pos_lse[:, None]), 0.0
        )
        slopes.append((row_weight[:, None] * spread * score_scale).astype(BF))
    mine = jnp.concatenate(slopes, axis=1)
    rows = row_group(mine, triple_swap(mine), u)
    full = all_rows(rows, triple_shift(rows, 1), triple_shift(rows, 2), v)
    near_full, far_full = full[:, : 2 * SEG], full[:, 2 * SEG :]

    far_back = core_swap(key_grad(far_full[:, SEG:], hidden).astype(BF))
    far_sum = key_grad(far_full[:, :SEG], hidden) + far_back.astype(F32)
    far_sum = far_sum.astype(BF)
    far_home = dp_shift(far_sum, -2)

    near_sum = after(key_grad(near_full[:, :SEG], hidden).astype(BF), far_sum)
    odd_sum = after(key_grad(near_full[:, SEG:], hidden).astype(BF), far_sum)
    near_home = dp_shift(near_sum, -4)
    odd_back = odd_home(odd_sum)
    near_full = after(near_full, far_home)
    query_grad = jnp.dot(near_full, near_keys, preferred_element_type=F32)
    query_grad = query_grad + jnp.dot(far_full, far_keys, preferred_element_type=F32)
    home = near_home.astype(F32) + odd_back.astype(F32) + far_home.astype(F32)
    return (query_grad + home).astype(BF)


def solution(mesh):
    placed = (P("dp", "tensor"), P("dp"), P("dp"), P("dp"), P("dp"), P("dp"))
    return jax.shard_map(
        per_device, mesh=mesh, in_specs=placed, out_specs=P("dp", "tensor"), check_vma=False
    )
```

```python
import math

import jax
import jax.numpy as jnp
from jax import lax
from jax.sharding import PartitionSpec as P

KW = 3840
SEG = 384
BF = jnp.bfloat16
F32 = jnp.float32


def dp_shift(value, steps):
    count = lax.axis_size("dp")
    return lax.ppermute(value, "dp", [(i, (i + steps) % count) for i in range(count)])


def core_swap(value):
    count = lax.axis_size("dp")
    return lax.ppermute(value, "dp", [(i, i ^ 1) for i in range(count)])


def odd_keys(value):
    count = lax.axis_size("dp")
    return lax.ppermute(value, "dp", [(i, (i + (1 if i % 2 == 0 else 3)) % count) for i in range(count)])


def odd_home(value):
    count = lax.axis_size("dp")
    return lax.ppermute(value, "dp", [((i + (1 if i % 2 == 0 else 3)) % count, i) for i in range(count)])


def triple_shift(value, steps):
    pairs = [(3 * u + v, 3 * u + (v + steps) % 3) for u in range(2) for v in range(3)]
    return lax.ppermute(value, "tensor", pairs)


def triple_swap(value):
    return lax.ppermute(value, "tensor", [(r, (r + 3) % 6) for r in range(6)])


def rows_of(value, start, size):
    return lax.dynamic_slice_in_dim(value, start, size, 0)


def partial_of(queries, keys):
    return lax.dot_general(queries, keys, (((1,), (1,)), ((), ())), preferred_element_type=F32)


def with_codes(hidden, targets, padding):
    code = jnp.where(padding == 1, targets + 1, 0)
    digits = jnp.stack([code >> 8, code & 255]).astype(BF)
    tail = jnp.pad(digits, ((0, 14), (0, hidden.shape[1] - SEG)))
    return jnp.concatenate([hidden, tail], axis=0)


def codes_of(payload):
    digits = lax.optimization_barrier(payload[SEG:])[:2, :SEG].astype(F32)
    return digits[0] * 256.0 + digits[1]


def after(value, *others):
    return lax.optimization_barrier((value,) + others)[0]


def outgoing(hidden, keys, v):
    return tuple(
        partial_of(rows_of(hidden, ((v + steps) % 3) * 128, 128), keys) for steps in (1, 2)
    )


def normalizer(parts, outside):
    peak = outside
    for scores, allowed in parts:
        peak = jnp.maximum(peak, jnp.max(jnp.where(allowed, scores, -1e30), axis=1))
    total = jnp.exp(outside - peak)
    for scores, allowed in parts:
        total = total + jnp.sum(jnp.where(allowed, jnp.exp(scores - peak[:, None]), 0.0), axis=1)
    return peak + jnp.log(total)


def gathered(mine, u, v):
    partner = triple_swap(mine)
    own = (triple_shift(mine, 1), triple_shift(mine, 2))
    partner, *own = lax.optimization_barrier((partner,) + own)
    passed = (triple_shift(partner, 1), triple_shift(partner, 2))
    full = jnp.zeros((SEG, mine.shape[1]), BF)
    for half, pieces in ((u, (mine, *own)), (1 - u, (partner, *passed))):
        for steps, piece in enumerate(pieces):
            start = ((v + 3 - steps) % 3) * 128 + half * 64
            full = lax.dynamic_update_slice_in_dim(full, piece, start, 0)
    return full


def key_grad(slopes, hidden):
    return lax.dot_general(slopes, hidden, (((0,), (0,)), ((), ())), preferred_element_type=F32)


def per_device(hidden, targets, padding, gold_logit, vocab_lse, cotangent):
    score_scale = 1.0 / math.sqrt(KW)
    core = lax.axis_index("dp") % 2
    r = lax.axis_index("tensor")
    u, v = r // 3, r % 3
    weight = cotangent * padding.astype(F32)
    payload = with_codes(hidden, targets, padding)

    far = dp_shift(payload, 2)
    near = dp_shift(payload, 4)
    odd = odd_keys(payload)
    pair_hidden = core_swap(after(hidden, odd))
    own_rows = rows_of(hidden, v * 128, 128)

    near_keys = jnp.concatenate([near[:SEG], odd[:SEG]], axis=0)
    near_codes = jnp.concatenate([codes_of(near), codes_of(odd)])
    near_out = outgoing(hidden, near_keys, v)
    near_out = lax.optimization_barrier(near_out + (far,))[:2]
    near_group = partial_of(own_rows, near_keys)
    near_in = (triple_shift(near_out[0], 1), triple_shift(near_out[1], 2))

    far_pair = core_swap(far)
    far_keys = jnp.concatenate([far[:SEG], far_pair[:SEG]], axis=0)
    far_codes = jnp.concatenate([codes_of(far), codes_of(far_pair)])
    far_out = outgoing(hidden, far_keys, v)
    near_group = near_group + after(near_in[0], *far_out) + near_in[1]
    near_other = triple_swap(rows_of(near_group, (1 - u) * 64, 64))
    far_group = partial_of(own_rows, far_keys)
    far_group = far_group + triple_shift(far_out[0], 1) + triple_shift(far_out[1], 2)
    far_other = triple_swap(rows_of(far_group, (1 - u) * 64, 64))
    near_scores = (rows_of(near_group, u * 64, 64) + near_other) * score_scale
    far_scores = (rows_of(far_group, u * 64, 64) + far_other) * score_scale

    base = v * 128 + u * 64
    row_codes = rows_of(targets, base, 64).astype(F32) + 1.0
    parts = []
    for scores, codes in ((near_scores, near_codes), (far_scores, far_codes)):
        usable = jnp.broadcast_to((codes > 0.0)[None], scores.shape)
        matches = usable & (codes[None] == row_codes[:, None])
        parts.append((scores, usable, matches))
    total_lse = normalizer([(s, a) for s, a, m in parts], rows_of(vocab_lse, base, 64))
    pos_lse = normalizer([(s, m) for s, a, m in parts], rows_of(gold_logit, base, 64))
    row_weight = rows_of(weight, base, 64)
    slopes = []
    for scores, usable, matches in parts:
        spread = jnp.where(usable, jnp.exp(scores - total_lse[:, None]), 0.0) - jnp.where(
            matches, jnp.exp(scores - pos_lse[:, None]), 0.0
        )
        slopes.append((row_weight[:, None] * spread * score_scale).astype(BF))
    mine = jnp.concatenate(slopes, axis=1)
    full = gathered(mine, u, v)
    near_full, far_full = full[:, : 2 * SEG], full[:, 2 * SEG :]

    pair_slopes = core_swap(far_full[:, SEG:])
    own_sum = lax.optimization_barrier(key_grad(far_full[:, :SEG], hidden))
    far_sum = own_sum + key_grad(pair_slopes, pair_hidden)
    far_sum = far_sum.astype(BF)
    far_home = dp_shift(far_sum, -2)

    near_sum = after(key_grad(near_full[:, :SEG], hidden).astype(BF), far_sum)
    odd_sum = after(key_grad(near_full[:, SEG:], hidden).astype(BF), far_sum)
    near_home = dp_shift(near_sum, -4)
    odd_back = odd_home(odd_sum)
    near_full = after(near_full, far_home)
    query_grad = jnp.dot(near_full, near_keys, preferred_element_type=F32)
    query_grad = query_grad + jnp.dot(far_full, far_keys, preferred_element_type=F32)
    home = near_home.astype(F32) + odd_back.astype(F32) + far_home.astype(F32)
    return (query_grad + home).astype(BF)


def solution(mesh):
    placed = (P("dp", "tensor"), P("dp"), P("dp"), P("dp"), P("dp"), P("dp"))
    return jax.shard_map(
        per_device, mesh=mesh, in_specs=placed, out_specs=P("dp", "tensor"), check_vma=False
    )
```

```python
import math

import jax
import jax.numpy as jnp
from jax import lax
from jax.sharding import PartitionSpec as P

KW = 3840
SEG = 384
BF = jnp.bfloat16
F32 = jnp.float32


def dp_shift(value, steps):
    count = lax.axis_size("dp")
    return lax.ppermute(value, "dp", [(i, (i + steps) % count) for i in range(count)])


def core_swap(value):
    count = lax.axis_size("dp")
    return lax.ppermute(value, "dp", [(i, i ^ 1) for i in range(count)])


def odd_keys(value):
    count = lax.axis_size("dp")
    return lax.ppermute(value, "dp", [(i, (i + (1 if i % 2 == 0 else 3)) % count) for i in range(count)])


def odd_home(value):
    count = lax.axis_size("dp")
    return lax.ppermute(value, "dp", [((i + (1 if i % 2 == 0 else 3)) % count, i) for i in range(count)])


def triple_shift(value, steps):
    pairs = [(3 * u + v, 3 * u + (v + steps) % 3) for u in range(2) for v in range(3)]
    return lax.ppermute(value, "tensor", pairs)


def pair_swap(value):
    return lax.ppermute(value, "tensor", [(r, r ^ 1) for r in range(6)])


def stride_shift(value, steps):
    pairs = [(2 * n + w, 2 * ((n + steps) % 3) + w) for n in range(3) for w in range(2)]
    return lax.ppermute(value, "tensor", pairs)


def triple_swap(value):
    return lax.ppermute(value, "tensor", [(r, (r + 3) % 6) for r in range(6)])


def rows_of(value, start, size):
    return lax.dynamic_slice_in_dim(value, start, size, 0)


def parity_rows(value, w):
    starts = [((w + 2 * n) % 3) * 128 + ((w + 2 * n) // 3) * 64 for n in range(3)]
    return jnp.concatenate([rows_of(value, start, 64) for start in starts], axis=0)


def partial_of(queries, keys):
    return lax.dot_general(queries, keys, (((1,), (1,)), ((), ())), preferred_element_type=F32)


def with_codes(hidden, targets, padding):
    code = jnp.where(padding == 1, targets + 1, 0)
    digits = jnp.stack([code >> 8, code & 255]).astype(BF)
    tail = jnp.pad(digits, ((0, 14), (0, hidden.shape[1] - SEG)))
    return jnp.concatenate([hidden, tail], axis=0)


def codes_of(payload):
    digits = lax.optimization_barrier(payload[SEG:])[:2, :SEG].astype(F32)
    return digits[0] * 256.0 + digits[1]


def after(value, *others):
    return lax.optimization_barrier((value,) + others)[0]


def outgoing(hidden, keys, v):
    return tuple(
        partial_of(rows_of(hidden, ((v + steps) % 3) * 128, 128), keys) for steps in (1, 2)
    )


def normalizer(parts, outside):
    peak = outside
    for scores, allowed in parts:
        peak = jnp.maximum(peak, jnp.max(jnp.where(allowed, scores, -1e30), axis=1))
    total = jnp.exp(outside - peak)
    for scores, allowed in parts:
        total = total + jnp.sum(jnp.where(allowed, jnp.exp(scores - peak[:, None]), 0.0), axis=1)
    return peak + jnp.log(total)


def gathered(mine, u, v):
    partner = triple_swap(mine)
    own = (triple_shift(mine, 1), triple_shift(mine, 2))
    partner, *own = lax.optimization_barrier((partner,) + own)
    passed = (triple_shift(partner, 1), triple_shift(partner, 2))
    full = jnp.zeros((SEG, mine.shape[1]), BF)
    for half, pieces in ((u, (mine, *own)), (1 - u, (partner, *passed))):
        for steps, piece in enumerate(pieces):
            start = ((v + 3 - steps) % 3) * 128 + half * 64
            full = lax.dynamic_update_slice_in_dim(full, piece, start, 0)
    return full


def key_grad(slopes, hidden):
    return lax.dot_general(slopes, hidden, (((0,), (0,)), ((), ())), preferred_element_type=F32)


def per_device(hidden, targets, padding, gold_logit, vocab_lse, cotangent):
    score_scale = 1.0 / math.sqrt(KW)
    core = lax.axis_index("dp") % 2
    r = lax.axis_index("tensor")
    u, v = r // 3, r % 3
    n, w = r // 2, r % 2
    weight = cotangent * padding.astype(F32)
    payload = with_codes(hidden, targets, padding)

    far = dp_shift(payload, 2)
    near = dp_shift(payload, 4)
    odd = odd_keys(payload)
    far_code = codes_of(far)
    near, odd = lax.optimization_barrier((near, odd, far_code))[:2]
    pair_hidden = core_swap(hidden)
    own_rows = rows_of(hidden, v * 128, 128)

    near_keys = jnp.concatenate([near[:SEG], odd[:SEG]], axis=0)
    near_codes = jnp.concatenate([codes_of(near), codes_of(odd)])
    near_out = partial_of(parity_rows(hidden, 1 - w), near_keys)
    near_in = pair_swap(near_out)

    far_pair = core_swap(far)
    far_keys = jnp.concatenate([far[:SEG], far_pair[:SEG]], axis=0)
    far_codes = jnp.concatenate([far_code, codes_of(far_pair)])
    far_out = outgoing(hidden, far_keys, v)
    near_group = partial_of(parity_rows(hidden, w), near_keys) + after(near_in, *far_out)
    near_one = stride_shift(rows_of(near_group, ((n + 1) % 3) * 64, 64), 1)
    near_two = stride_shift(rows_of(near_group, ((n + 2) % 3) * 64, 64), 2)
    far_group = partial_of(own_rows, far_keys)
    far_group = far_group + triple_shift(far_out[0], 1) + triple_shift(far_out[1], 2)
    far_other = triple_swap(rows_of(far_group, (1 - u) * 64, 64))
    near_scores = (rows_of(near_group, n * 64, 64) + near_one + near_two) * score_scale
    far_scores = (rows_of(far_group, u * 64, 64) + far_other) * score_scale

    base = v * 128 + u * 64
    row_codes = rows_of(targets, base, 64).astype(F32) + 1.0
    parts = []
    for scores, codes in ((near_scores, near_codes), (far_scores, far_codes)):
        usable = jnp.broadcast_to((codes > 0.0)[None], scores.shape)
        matches = usable & (codes[None] == row_codes[:, None])
        parts.append((scores, usable, matches))
    total_lse = normalizer([(s, a) for s, a, m in parts], rows_of(vocab_lse, base, 64))
    pos_lse = normalizer([(s, m) for s, a, m in parts], rows_of(gold_logit, base, 64))
    row_weight = rows_of(weight, base, 64)
    slopes = []
    for scores, usable, matches in parts:
        spread = jnp.where(usable, jnp.exp(scores - total_lse[:, None]), 0.0) - jnp.where(
            matches, jnp.exp(scores - pos_lse[:, None]), 0.0
        )
        slopes.append((row_weight[:, None] * spread * score_scale).astype(BF))
    mine = jnp.concatenate(slopes, axis=1)
    full = gathered(mine, u, v)
    near_full, far_full = full[:, : 2 * SEG], full[:, 2 * SEG :]

    pair_slopes = core_swap(far_full[:, SEG:])
    own_sum = lax.optimization_barrier(key_grad(far_full[:, :SEG], hidden))
    far_sum = own_sum + key_grad(pair_slopes, pair_hidden)
    far_sum = far_sum.astype(BF)
    far_home = dp_shift(far_sum, -2)

    near_sum = after(key_grad(near_full[:, :SEG], hidden).astype(BF), far_sum)
    odd_sum = after(key_grad(near_full[:, SEG:], hidden).astype(BF), far_sum)
    near_home = dp_shift(near_sum, -4)
    odd_back = odd_home(odd_sum)
    near_full = after(near_full, far_home)
    query_grad = jnp.dot(near_full, near_keys, preferred_element_type=F32)
    query_grad = query_grad + jnp.dot(far_full, far_keys, preferred_element_type=F32)
    home = near_home.astype(F32) + odd_back.astype(F32) + far_home.astype(F32)
    return (query_grad + home).astype(BF)


def solution(mesh):
    placed = (P("dp", "tensor"), P("dp"), P("dp"), P("dp"), P("dp"), P("dp"))
    return jax.shard_map(
        per_device, mesh=mesh, in_specs=placed, out_specs=P("dp", "tensor"), check_vma=False
    )
```

```python
import math

import jax
import jax.numpy as jnp
from jax import lax
from jax.sharding import PartitionSpec as P

KW = 3840
SEG = 384
BF = jnp.bfloat16
F32 = jnp.float32


def dp_shift(value, steps):
    count = lax.axis_size("dp")
    return lax.ppermute(value, "dp", [(i, (i + steps) % count) for i in range(count)])


def core_swap(value):
    count = lax.axis_size("dp")
    return lax.ppermute(value, "dp", [(i, i ^ 1) for i in range(count)])


def odd_keys(value):
    count = lax.axis_size("dp")
    return lax.ppermute(value, "dp", [(i, (i + (1 if i % 2 == 0 else 3)) % count) for i in range(count)])


def odd_home(value):
    count = lax.axis_size("dp")
    return lax.ppermute(value, "dp", [((i + (1 if i % 2 == 0 else 3)) % count, i) for i in range(count)])


def triple_shift(value, steps):
    pairs = [(3 * u + v, 3 * u + (v + steps) % 3) for u in range(2) for v in range(3)]
    return lax.ppermute(value, "tensor", pairs)


def pair_swap(value):
    return lax.ppermute(value, "tensor", [(r, r ^ 1) for r in range(6)])


def stride_shift(value, steps):
    pairs = [(2 * n + w, 2 * ((n + steps) % 3) + w) for n in range(3) for w in range(2)]
    return lax.ppermute(value, "tensor", pairs)


def triple_swap(value):
    return lax.ppermute(value, "tensor", [(r, (r + 3) % 6) for r in range(6)])


def rows_of(value, start, size):
    return lax.dynamic_slice_in_dim(value, start, size, 0)


def parity_rows(value, w):
    starts = [((w + 2 * n) % 3) * 128 + ((w + 2 * n) // 3) * 64 for n in range(3)]
    return jnp.concatenate([rows_of(value, start, 64) for start in starts], axis=0)


def partial_of(queries, keys):
    return lax.dot_general(queries, keys, (((1,), (1,)), ((), ())), preferred_element_type=F32)


def with_codes(hidden, targets, padding):
    code = jnp.where(padding == 1, targets + 1, 0)
    digits = jnp.stack([code >> 8, code & 255]).astype(BF)
    tail = jnp.pad(digits, ((0, 14), (0, hidden.shape[1] - SEG)))
    return jnp.concatenate([hidden, tail], axis=0)


def codes_of(payload):
    digits = lax.optimization_barrier(payload[SEG:])[:2, :SEG].astype(F32)
    return digits[0] * 256.0 + digits[1]


def after(value, *others):
    return lax.optimization_barrier((value,) + others)[0]


def outgoing(hidden, keys, v):
    return tuple(
        partial_of(rows_of(hidden, ((v + steps) % 3) * 128, 128), keys) for steps in (1, 2)
    )


def normalizer(parts, outside):
    peak = outside
    for scores, allowed in parts:
        peak = jnp.maximum(peak, jnp.max(jnp.where(allowed, scores, -1e30), axis=1))
    total = jnp.exp(outside - peak)
    for scores, allowed in parts:
        total = total + jnp.sum(jnp.where(allowed, jnp.exp(scores - peak[:, None]), 0.0), axis=1)
    return peak + jnp.log(total)


def gathered(mine, u, v):
    partner = triple_swap(mine)
    own = (triple_shift(mine, 1), triple_shift(mine, 2))
    partner, *own = lax.optimization_barrier((partner,) + own)
    passed = (triple_shift(partner, 1), triple_shift(partner, 2))
    full = jnp.zeros((SEG, mine.shape[1]), BF)
    for half, pieces in ((u, (mine, *own)), (1 - u, (partner, *passed))):
        for steps, piece in enumerate(pieces):
            start = ((v + 3 - steps) % 3) * 128 + half * 64
            full = lax.dynamic_update_slice_in_dim(full, piece, start, 0)
    return full


def key_grad(slopes, hidden):
    return lax.dot_general(slopes, hidden, (((0,), (0,)), ((), ())), preferred_element_type=F32)


def per_device(hidden, targets, padding, gold_logit, vocab_lse, cotangent):
    score_scale = 1.0 / math.sqrt(KW)
    core = lax.axis_index("dp") % 2
    r = lax.axis_index("tensor")
    u, v = r // 3, r % 3
    n, w = r // 2, r % 2
    weight = cotangent * padding.astype(F32)
    payload = with_codes(hidden, targets, padding)

    far = dp_shift(payload, 2)
    near = dp_shift(payload, 4)
    odd = odd_keys(payload)
    far_code = codes_of(far)
    pair_hidden = core_swap(hidden)
    own_rows = rows_of(hidden, v * 128, 128)

    near_keys = jnp.concatenate([near[:SEG], odd[:SEG]], axis=0)
    near_codes = jnp.concatenate([codes_of(near), codes_of(odd)])
    near_out = partial_of(parity_rows(hidden, 1 - w), near_keys)
    near_in = pair_swap(near_out)

    near_group = partial_of(parity_rows(hidden, w), near_keys) + near_in
    far_pair = core_swap(far)
    far_keys = jnp.concatenate([far[:SEG], far_pair[:SEG]], axis=0)
    far_codes = jnp.concatenate([far_code, codes_of(far_pair)])
    far_keys, near_group = lax.optimization_barrier((far_keys, near_group))
    far_out = outgoing(hidden, far_keys, v)
    near_one = stride_shift(rows_of(near_group, ((n + 1) % 3) * 64, 64), 1)
    near_two = stride_shift(rows_of(near_group, ((n + 2) % 3) * 64, 64), 2)
    far_group = partial_of(own_rows, far_keys)
    far_group = far_group + triple_shift(far_out[0], 1) + triple_shift(far_out[1], 2)
    far_other = triple_swap(rows_of(far_group, (1 - u) * 64, 64))
    near_scores = (rows_of(near_group, n * 64, 64) + near_one + near_two) * score_scale
    far_scores = (rows_of(far_group, u * 64, 64) + far_other) * score_scale

    base = v * 128 + u * 64
    row_codes = rows_of(targets, base, 64).astype(F32) + 1.0
    parts = []
    for scores, codes in ((near_scores, near_codes), (far_scores, far_codes)):
        usable = jnp.broadcast_to((codes > 0.0)[None], scores.shape)
        matches = usable & (codes[None] == row_codes[:, None])
        parts.append((scores, usable, matches))
    total_lse = normalizer([(s, a) for s, a, m in parts], rows_of(vocab_lse, base, 64))
    pos_lse = normalizer([(s, m) for s, a, m in parts], rows_of(gold_logit, base, 64))
    row_weight = rows_of(weight, base, 64)
    slopes = []
    for scores, usable, matches in parts:
        spread = jnp.where(usable, jnp.exp(scores - total_lse[:, None]), 0.0) - jnp.where(
            matches, jnp.exp(scores - pos_lse[:, None]), 0.0
        )
        slopes.append((row_weight[:, None] * spread * score_scale).astype(BF))
    mine = jnp.concatenate(slopes, axis=1)
    full = gathered(mine, u, v)
    near_full, far_full = full[:, : 2 * SEG], full[:, 2 * SEG :]

    pair_slopes = core_swap(far_full[:, SEG:])
    own_sum = lax.optimization_barrier(key_grad(far_full[:, :SEG], hidden))
    far_sum = own_sum + key_grad(pair_slopes, pair_hidden)
    far_sum = far_sum.astype(BF)
    far_home = dp_shift(far_sum, -2)

    near_sum = after(key_grad(near_full[:, :SEG], hidden).astype(BF), far_sum)
    odd_sum = after(key_grad(near_full[:, SEG:], hidden).astype(BF), far_sum)
    near_home = dp_shift(near_sum, -4)
    odd_back = odd_home(odd_sum)
    near_full = after(near_full, far_home)
    query_grad = jnp.dot(near_full, near_keys, preferred_element_type=F32)
    query_grad = query_grad + jnp.dot(far_full, far_keys, preferred_element_type=F32)
    home = near_home.astype(F32) + odd_back.astype(F32) + far_home.astype(F32)
    return (query_grad + home).astype(BF)


def solution(mesh):
    placed = (P("dp", "tensor"), P("dp"), P("dp"), P("dp"), P("dp"), P("dp"))
    return jax.shard_map(
        per_device, mesh=mesh, in_specs=placed, out_specs=P("dp", "tensor"), check_vma=False
    )
```

```python
import math

import jax
import jax.numpy as jnp
from jax import lax
from jax.sharding import PartitionSpec as P

KW = 3840
SEG = 384
BF = jnp.bfloat16
F32 = jnp.float32


def dp_permute(value, pairs):
    return lax.ppermute(value, "dp", pairs)


def core_swap(value):
    return dp_permute(value, [(i, i ^ 1) for i in range(lax.axis_size("dp"))])


def first_keys():
    count = lax.axis_size("dp")
    return [(i, (i + (4 if i % 2 == 0 else 2)) % count) for i in range(count)]


def second_keys():
    count = lax.axis_size("dp")
    return [(i, (i + 3) % count) for i in range(count)]


def reverse(pairs):
    return [(target, source) for source, target in pairs]


def triple_shift(value, steps):
    pairs = [(3 * u + v, 3 * u + (v + steps) % 3) for u in range(2) for v in range(3)]
    return lax.ppermute(value, "tensor", pairs)


def triple_swap(value):
    return lax.ppermute(value, "tensor", [(r, (r + 3) % 6) for r in range(6)])


def rows_of(value, start, size, axis=0):
    return lax.dynamic_slice_in_dim(value, start, size, axis)


def partial_of(queries, keys):
    return lax.dot_general(queries, keys, (((1,), (1,)), ((), ())), preferred_element_type=F32)


def key_grad(slopes, hidden):
    return lax.dot_general(slopes, hidden, (((0,), (0,)), ((), ())), preferred_element_type=F32)


def with_codes(hidden, targets, padding):
    code = jnp.where(padding == 1, targets + 1, 0)
    digits = jnp.stack([code >> 8, code & 255]).astype(BF)
    tail = jnp.pad(digits, ((0, 14), (0, hidden.shape[1] - SEG)))
    return jnp.concatenate([hidden, tail], axis=0)


def codes_of(payload):
    digits = lax.optimization_barrier(payload[SEG:])[:2, :SEG].astype(F32)
    return digits[0] * 256.0 + digits[1]


def summed_part(scores, allowed, outside):
    peak = jnp.maximum(outside, jnp.max(jnp.where(allowed, scores, -1e30), axis=2))
    return peak, jnp.sum(jnp.where(allowed, jnp.exp(scores - peak[..., None]), 0.0), axis=2)


def joined_lse(outside, mine, other):
    peak = jnp.maximum(mine[0], other[0])
    total = mine[1] * jnp.exp(mine[0] - peak) + other[1] * jnp.exp(other[0] - peak)
    return peak + jnp.log(jnp.exp(outside - peak) + total)


def gathered(mine, u, v):
    partner = triple_swap(mine)
    own = (triple_shift(mine, 1), triple_shift(mine, 2))
    partner, *own = lax.optimization_barrier((partner,) + own)
    passed = (triple_shift(partner, 1), triple_shift(partner, 2))
    full = jnp.zeros((2, SEG, mine.shape[2]), BF)
    for half, pieces in ((u, (mine, *own)), (1 - u, (partner, *passed))):
        for steps, piece in enumerate(pieces):
            start = ((v + 3 - steps) % 3) * 128 + half * 64
            full = lax.dynamic_update_slice_in_dim(full, piece, start, 1)
    return full


def per_device(hidden, targets, padding, gold_logit, vocab_lse, cotangent):
    score_scale = 1.0 / math.sqrt(KW)
    core = lax.axis_index("dp") % 2
    r = lax.axis_index("tensor")
    u, v = r // 3, r % 3
    payload = with_codes(hidden, targets, padding)

    key_one = dp_permute(payload, first_keys())
    key_two = dp_permute(payload, second_keys())
    pair_hidden = core_swap(payload)[:SEG]
    weight = cotangent * padding.astype(F32)
    row_data = jnp.stack([targets.astype(F32) + 1.0, gold_logit, vocab_lse, weight])
    row_data = rows_of(row_data, v * 128 + u * 64, 64, 1)
    row_data = jnp.stack([row_data, core_swap(row_data)])
    row_codes, gold, vocab, weight = (row_data[:, i] for i in range(4))

    key_own = jnp.where(core == 0, payload, key_one)
    keys = [
        jnp.concatenate([key_one[:SEG], key_two[:SEG]], axis=0),
        jnp.concatenate([key_own[:SEG], key_two[:SEG]], axis=0),
    ]
    code_two = codes_of(key_two)
    codes = jnp.stack(
        [
            jnp.concatenate([codes_of(key_one), code_two]),
            jnp.concatenate([codes_of(key_own), code_two]),
        ]
    )

    def partial(steps):
        start = ((v + steps) % 3) * 128
        return jnp.stack(
            [
                partial_of(rows_of(queries, start, 128), read)
                for queries, read in zip((hidden, pair_hidden), keys)
            ]
        )

    first = triple_shift(partial(1), 1)
    second = triple_shift(partial(2), 2)
    group = partial(0) + first + second
    other_half = triple_swap(rows_of(group, (1 - u) * 64, 64, 1))
    scores = (rows_of(group, u * 64, 64, 1) + other_half) * score_scale

    usable = jnp.broadcast_to((codes > 0.0)[:, None], scores.shape)
    matches = usable & (codes[:, None] == row_codes[:, :, None])
    total_part = summed_part(scores, usable, vocab)
    pos_part = summed_part(scores, matches, gold)
    stats = jnp.stack([*total_part, *pos_part], axis=1)
    other = core_swap(stats)
    other = jnp.concatenate([other[1:], other[:1]], axis=0)
    total_lse = joined_lse(vocab, total_part, (other[:, 0], other[:, 1]))
    pos_lse = joined_lse(gold, pos_part, (other[:, 2], other[:, 3]))
    spread = jnp.where(usable, jnp.exp(scores - total_lse[..., None]), 0.0) - jnp.where(
        matches, jnp.exp(scores - pos_lse[..., None]), 0.0
    )
    slopes = gathered((weight[..., None] * spread * score_scale).astype(BF), u, v)

    both_hidden = jnp.concatenate([hidden, pair_hidden], axis=0)
    flat = slopes.reshape(2 * SEG, 2 * SEG)
    grad_two = key_grad(flat[:, SEG:], both_hidden).astype(BF)
    home_two = dp_permute(grad_two, reverse(second_keys()))
    pair_one = key_grad(slopes[1, :, :SEG], pair_hidden)
    grad_one = key_grad(slopes[0, :, :SEG], hidden) + jnp.where(core == 1, pair_one, 0.0)
    home_one = dp_permute(grad_one.astype(BF), reverse(first_keys()))
    pair_grad = core_swap(jnp.dot(slopes[1], keys[1], preferred_element_type=F32).astype(BF))
    own_grad = jnp.dot(slopes[0], keys[0], preferred_element_type=F32)
    own_grad = own_grad + jnp.where(core == 0, pair_one, 0.0)
    home = home_one.astype(F32) + home_two.astype(F32) + pair_grad.astype(F32)
    return (own_grad + home).astype(BF)


def solution(mesh):
    placed = (P("dp", "tensor"), P("dp"), P("dp"), P("dp"), P("dp"), P("dp"))
    return jax.shard_map(
        per_device, mesh=mesh, in_specs=placed, out_specs=P("dp", "tensor"), check_vma=False
    )
```

```python
import math

import jax
import jax.numpy as jnp
from jax import lax
from jax.sharding import PartitionSpec as P

KW = 3840
SEG = 384
BF = jnp.bfloat16
F32 = jnp.float32


def dp_permute(value, pairs):
    return lax.ppermute(value, "dp", pairs)


def core_swap(value):
    return dp_permute(value, [(i, i ^ 1) for i in range(lax.axis_size("dp"))])


def first_keys():
    count = lax.axis_size("dp")
    return [(i, (i + (4 if i % 2 == 0 else 2)) % count) for i in range(count)]


def second_keys():
    count = lax.axis_size("dp")
    return [(i, (i + 3) % count) for i in range(count)]


def reverse(pairs):
    return [(target, source) for source, target in pairs]


def triple_shift(value, steps):
    pairs = [(3 * u + v, 3 * u + (v + steps) % 3) for u in range(2) for v in range(3)]
    return lax.ppermute(value, "tensor", pairs)


def triple_swap(value):
    return lax.ppermute(value, "tensor", [(r, (r + 3) % 6) for r in range(6)])


def rows_of(value, start, size, axis=0):
    return lax.dynamic_slice_in_dim(value, start, size, axis)


def partial_of(queries, keys):
    return lax.dot_general(queries, keys, (((1,), (1,)), ((), ())), preferred_element_type=F32)


def key_grad(slopes, hidden):
    return lax.dot_general(slopes, hidden, (((0,), (0,)), ((), ())), preferred_element_type=F32)


def with_codes(hidden, targets, padding):
    code = jnp.where(padding == 1, targets + 1, 0)
    digits = jnp.stack([code >> 8, code & 255]).astype(BF)
    tail = jnp.pad(digits, ((0, 14), (0, hidden.shape[1] - SEG)))
    return jnp.concatenate([hidden, tail], axis=0)


def codes_of(payload):
    digits = lax.optimization_barrier(payload[SEG:])[:2, :SEG].astype(F32)
    return digits[0] * 256.0 + digits[1]


def summed_part(scores, allowed, outside):
    peak = jnp.maximum(outside, jnp.max(jnp.where(allowed, scores, -1e30), axis=2))
    return peak, jnp.sum(jnp.where(allowed, jnp.exp(scores - peak[..., None]), 0.0), axis=2)


def joined_lse(outside, mine, other):
    peak = jnp.maximum(mine[0], other[0])
    total = mine[1] * jnp.exp(mine[0] - peak) + other[1] * jnp.exp(other[0] - peak)
    return peak + jnp.log(jnp.exp(outside - peak) + total)


def gathered(mine, u, v):
    partner = triple_swap(mine)
    own = (triple_shift(mine, 1), triple_shift(mine, 2))
    partner, *own = lax.optimization_barrier((partner,) + own)
    passed = (triple_shift(partner, 1), triple_shift(partner, 2))
    full = jnp.zeros((2, SEG, mine.shape[2]), BF)
    for half, pieces in ((u, (mine, *own)), (1 - u, (partner, *passed))):
        for steps, piece in enumerate(pieces):
            start = ((v + 3 - steps) % 3) * 128 + half * 64
            full = lax.dynamic_update_slice_in_dim(full, piece, start, 1)
    return full


def per_device(hidden, targets, padding, gold_logit, vocab_lse, cotangent):
    score_scale = 1.0 / math.sqrt(KW)
    core = lax.axis_index("dp") % 2
    r = lax.axis_index("tensor")
    u, v = r // 3, r % 3
    payload = with_codes(hidden, targets, padding)

    key_one = dp_permute(payload, first_keys())
    key_two = dp_permute(payload, second_keys())
    pair_hidden = core_swap(payload)[:SEG]
    weight = cotangent * padding.astype(F32)
    row_data = jnp.stack([targets.astype(F32) + 1.0, gold_logit, vocab_lse, weight])
    row_data = rows_of(row_data, v * 128 + u * 64, 64, 1)
    row_data = jnp.stack([row_data, core_swap(row_data)])
    row_codes, gold, vocab, weight = (row_data[:, i] for i in range(4))

    key_own = jnp.where(core == 0, payload, key_one)
    keys = [
        jnp.concatenate([key_one[:SEG], key_two[:SEG]], axis=0),
        jnp.concatenate([key_own[:SEG], key_two[:SEG]], axis=0),
    ]
    code_two = codes_of(key_two)
    codes = jnp.stack(
        [
            jnp.concatenate([codes_of(key_one), code_two]),
            jnp.concatenate([codes_of(key_own), code_two]),
        ]
    )

    def partial(queries, steps, half):
        start = ((v + steps) % 3) * 128 + half * 64
        parts = [partial_of(rows_of(q, start, 64), read) for q, read in zip(queries, keys)]
        return jnp.stack(parts)

    queries = (hidden, pair_hidden)
    sent = tuple(partial(queries, steps, 1 - u) for steps in (1, 2))
    *sent, own, pair = lax.optimization_barrier(sent + queries)
    queries = (own, pair)
    passing = partial(queries, 0, 1 - u) + triple_shift(sent[0], 1) + triple_shift(sent[1], 2)
    late = tuple(partial(queries, steps, u) for steps in (1, 2))
    passing, *late = lax.optimization_barrier((passing,) + late)
    from_partner = triple_swap(passing)
    scores = partial(queries, 0, u) + triple_shift(late[0], 1) + triple_shift(late[1], 2)
    scores = (scores + from_partner) * score_scale

    usable = jnp.broadcast_to((codes > 0.0)[:, None], scores.shape)
    matches = usable & (codes[:, None] == row_codes[:, :, None])
    total_part = summed_part(scores, usable, vocab)
    pos_part = summed_part(scores, matches, gold)
    stats = jnp.stack([*total_part, *pos_part], axis=1)
    other = core_swap(stats)
    other = jnp.concatenate([other[1:], other[:1]], axis=0)
    total_lse = joined_lse(vocab, total_part, (other[:, 0], other[:, 1]))
    pos_lse = joined_lse(gold, pos_part, (other[:, 2], other[:, 3]))
    spread = jnp.where(usable, jnp.exp(scores - total_lse[..., None]), 0.0) - jnp.where(
        matches, jnp.exp(scores - pos_lse[..., None]), 0.0
    )
    slopes = gathered((weight[..., None] * spread * score_scale).astype(BF), u, v)

    both_hidden = jnp.concatenate([hidden, pair_hidden], axis=0)
    flat = slopes.reshape(2 * SEG, 2 * SEG)
    grad_two = key_grad(flat[:, SEG:], both_hidden).astype(BF)
    home_two = dp_permute(grad_two, reverse(second_keys()))
    pair_one = key_grad(slopes[1, :, :SEG], pair_hidden)
    grad_one = key_grad(slopes[0, :, :SEG], hidden) + jnp.where(core == 1, pair_one, 0.0)
    home_one = dp_permute(grad_one.astype(BF), reverse(first_keys()))
    pair_grad = core_swap(jnp.dot(slopes[1], keys[1], preferred_element_type=F32).astype(BF))
    own_grad = jnp.dot(slopes[0], keys[0], preferred_element_type=F32)
    own_grad = own_grad + jnp.where(core == 0, pair_one, 0.0)
    home = home_one.astype(F32) + home_two.astype(F32) + pair_grad.astype(F32)
    return (own_grad + home).astype(BF)


def solution(mesh):
    placed = (P("dp", "tensor"), P("dp"), P("dp"), P("dp"), P("dp"), P("dp"))
    return jax.shard_map(
        per_device, mesh=mesh, in_specs=placed, out_specs=P("dp", "tensor"), check_vma=False
    )
```

```python
import math

import jax
import jax.numpy as jnp
from jax import lax
from jax.sharding import PartitionSpec as P

KW = 3840
SEG = 384
BF = jnp.bfloat16
F32 = jnp.float32


def dp_permute(value, pairs):
    return lax.ppermute(value, "dp", pairs)


def core_swap(value):
    return dp_permute(value, [(i, i ^ 1) for i in range(lax.axis_size("dp"))])


def first_keys():
    count = lax.axis_size("dp")
    return [(i, (i + (4 if i % 2 == 0 else 2)) % count) for i in range(count)]


def second_keys():
    count = lax.axis_size("dp")
    return [(i, (i + 3) % count) for i in range(count)]


def reverse(pairs):
    return [(target, source) for source, target in pairs]


def triple_shift(value, steps):
    pairs = [(3 * u + v, 3 * u + (v + steps) % 3) for u in range(2) for v in range(3)]
    return lax.ppermute(value, "tensor", pairs)


def triple_swap(value):
    return lax.ppermute(value, "tensor", [(r, (r + 3) % 6) for r in range(6)])


def rows_of(value, start, size, axis=0):
    return lax.dynamic_slice_in_dim(value, start, size, axis)


def partial_of(queries, keys):
    return lax.dot_general(queries, keys, (((1,), (1,)), ((), ())), preferred_element_type=F32)


def key_grad(slopes, hidden):
    return lax.dot_general(slopes, hidden, (((0,), (0,)), ((), ())), preferred_element_type=F32)


def with_codes(hidden, targets, padding):
    code = jnp.where(padding == 1, targets + 1, 0)
    digits = jnp.stack([code >> 8, code & 255]).astype(BF)
    tail = jnp.pad(digits, ((0, 14), (0, hidden.shape[1] - SEG)))
    return jnp.concatenate([hidden, tail], axis=0)


def codes_of(payload):
    digits = lax.optimization_barrier(payload[SEG:])[:2, :SEG].astype(F32)
    return digits[0] * 256.0 + digits[1]


def summed_part(scores, allowed, outside):
    peak = jnp.maximum(outside, jnp.max(jnp.where(allowed, scores, -1e30), axis=2))
    return peak, jnp.sum(jnp.where(allowed, jnp.exp(scores - peak[..., None]), 0.0), axis=2)


def joined_lse(outside, mine, other):
    peak = jnp.maximum(mine[0], other[0])
    total = mine[1] * jnp.exp(mine[0] - peak) + other[1] * jnp.exp(other[0] - peak)
    return peak + jnp.log(jnp.exp(outside - peak) + total)


def gathered(mine, u, v):
    partner = triple_swap(mine)
    own = (triple_shift(mine, 1), triple_shift(mine, 2))
    partner, *own = lax.optimization_barrier((partner,) + own)
    passed = (triple_shift(partner, 1), triple_shift(partner, 2))
    full = jnp.zeros((2, SEG, mine.shape[2]), BF)
    for half, pieces in ((u, (mine, *own)), (1 - u, (partner, *passed))):
        for steps, piece in enumerate(pieces):
            start = ((v + 3 - steps) % 3) * 128 + half * 64
            full = lax.dynamic_update_slice_in_dim(full, piece, start, 1)
    return full


def per_device(hidden, targets, padding, gold_logit, vocab_lse, cotangent):
    score_scale = 1.0 / math.sqrt(KW)
    core = lax.axis_index("dp") % 2
    r = lax.axis_index("tensor")
    u, v = r // 3, r % 3
    payload = with_codes(hidden, targets, padding)

    key_one = dp_permute(payload, first_keys())
    key_two = dp_permute(payload, second_keys())
    weight = cotangent * padding.astype(F32)
    row_data = jnp.stack([targets.astype(F32) + 1.0, gold_logit, vocab_lse, weight])
    row_data = rows_of(row_data, v * 128 + u * 64, 64, 1)
    row_data, late_payload = lax.optimization_barrier((row_data, payload))
    pair_hidden = core_swap(late_payload)[:SEG]
    row_data = jnp.stack([row_data, core_swap(row_data)])
    row_codes, gold, vocab, weight = (row_data[:, i] for i in range(4))

    key_own = jnp.where(core == 0, payload, key_one)
    key_own, key_two = lax.optimization_barrier((key_own, key_two))
    keys = [
        jnp.concatenate([key_one[:SEG], key_two[:SEG]], axis=0),
        jnp.concatenate([key_own[:SEG], key_two[:SEG]], axis=0),
    ]
    code_two = codes_of(key_two)
    codes = jnp.stack(
        [
            jnp.concatenate([codes_of(key_one), code_two]),
            jnp.concatenate([codes_of(key_own), code_two]),
        ]
    )

    def partial(queries, steps, half):
        start = ((v + steps) % 3) * 128 + half * 64
        parts = [partial_of(rows_of(q, start, 64), read) for q, read in zip(queries, keys)]
        return jnp.stack(parts)

    read_rows = [rows_of(hidden, ((v + steps) % 3) * 128 + (1 - u) * 64, 64) for steps in (1, 2)]
    own_sent = tuple(partial_of(rows, keys[0]) for rows in read_rows)
    *own_sent, pair_hidden = lax.optimization_barrier(own_sent + (pair_hidden,))
    sent = tuple(
        jnp.stack([mine, partial_of(rows_of(pair_hidden, start, 64), keys[1])])
        for mine, start in zip(own_sent, [((v + steps) % 3) * 128 + (1 - u) * 64 for steps in (1, 2)])
    )
    *sent, own, pair = lax.optimization_barrier(sent + (hidden, pair_hidden))
    queries = (own, pair)
    passing = partial(queries, 0, 1 - u) + triple_shift(sent[0], 1) + triple_shift(sent[1], 2)
    late = tuple(partial(queries, steps, u) for steps in (1, 2))
    passing, *late = lax.optimization_barrier((passing,) + late)
    from_partner = triple_swap(passing)
    scores = partial(queries, 0, u) + triple_shift(late[0], 1) + triple_shift(late[1], 2)
    scores = (scores + from_partner) * score_scale

    usable = jnp.broadcast_to((codes > 0.0)[:, None], scores.shape)
    matches = usable & (codes[:, None] == row_codes[:, :, None])
    total_part = summed_part(scores, usable, vocab)
    pos_part = summed_part(scores, matches, gold)
    stats = jnp.stack([*total_part, *pos_part], axis=1)
    other = core_swap(stats)
    other = jnp.concatenate([other[1:], other[:1]], axis=0)
    total_lse = joined_lse(vocab, total_part, (other[:, 0], other[:, 1]))
    pos_lse = joined_lse(gold, pos_part, (other[:, 2], other[:, 3]))
    spread = jnp.where(usable, jnp.exp(scores - total_lse[..., None]), 0.0) - jnp.where(
        matches, jnp.exp(scores - pos_lse[..., None]), 0.0
    )
    slopes = gathered((weight[..., None] * spread * score_scale).astype(BF), u, v)

    both_hidden = jnp.concatenate([hidden, pair_hidden], axis=0)
    flat = slopes.reshape(2 * SEG, 2 * SEG)
    pair_one = key_grad(slopes[1, :, :SEG], pair_hidden)
    grad_one = key_grad(slopes[0, :, :SEG], hidden) + jnp.where(core == 1, pair_one, 0.0)
    grad_one, flat = lax.optimization_barrier((grad_one.astype(BF), flat))
    home_one = dp_permute(grad_one, reverse(first_keys()))
    grad_two = key_grad(flat[:, SEG:], both_hidden).astype(BF)
    grad_two, flat = lax.optimization_barrier((grad_two, flat))
    home_two = dp_permute(grad_two, reverse(second_keys()))
    pair_grad = core_swap(jnp.dot(flat[SEG:], keys[1], preferred_element_type=F32).astype(BF))
    own_grad = jnp.dot(flat[:SEG], keys[0], preferred_element_type=F32)
    own_grad = lax.optimization_barrier(own_grad + jnp.where(core == 0, pair_one, 0.0))
    own_grad = lax.optimization_barrier(own_grad + home_one.astype(F32))
    own_grad = lax.optimization_barrier(own_grad + home_two.astype(F32))
    return (own_grad + pair_grad.astype(F32)).astype(BF)


def solution(mesh):
    placed = (P("dp", "tensor"), P("dp"), P("dp"), P("dp"), P("dp"), P("dp"))
    return jax.shard_map(
        per_device, mesh=mesh, in_specs=placed, out_specs=P("dp", "tensor"), check_vma=False
    )
```

```python
import math

import jax
import jax.numpy as jnp
from jax import lax
from jax.sharding import PartitionSpec as P

KW = 3840
SEG = 384
BF = jnp.bfloat16
F32 = jnp.float32


def dp_permute(value, pairs):
    return lax.ppermute(value, "dp", pairs)


def core_swap(value):
    return dp_permute(value, [(i, i ^ 1) for i in range(lax.axis_size("dp"))])


def first_keys():
    count = lax.axis_size("dp")
    return [(i, (i + (4 if i % 2 == 0 else 2)) % count) for i in range(count)]


def second_keys():
    count = lax.axis_size("dp")
    return [(i, (i + 3) % count) for i in range(count)]


def reverse(pairs):
    return [(target, source) for source, target in pairs]


def triple_shift(value, steps):
    pairs = [(3 * u + v, 3 * u + (v + steps) % 3) for u in range(2) for v in range(3)]
    return lax.ppermute(value, "tensor", pairs)


def triple_swap(value):
    return lax.ppermute(value, "tensor", [(r, (r + 3) % 6) for r in range(6)])


def rows_of(value, start, size, axis=0):
    return lax.dynamic_slice_in_dim(value, start, size, axis)


def partial_of(queries, keys):
    return lax.dot_general(queries, keys, (((1,), (1,)), ((), ())), preferred_element_type=F32)


def key_grad(slopes, hidden):
    return lax.dot_general(slopes, hidden, (((0,), (0,)), ((), ())), preferred_element_type=F32)


def with_codes(hidden, targets, padding):
    code = jnp.where(padding == 1, targets + 1, 0)
    digits = jnp.stack([code >> 8, code & 255]).astype(BF)
    tail = jnp.pad(digits, ((0, 14), (0, hidden.shape[1] - SEG)))
    return jnp.concatenate([hidden, tail], axis=0)


def codes_of(payload):
    digits = lax.optimization_barrier(payload[SEG:])[:2, :SEG].astype(F32)
    return digits[0] * 256.0 + digits[1]


def summed_part(scores, allowed, outside):
    peak = jnp.maximum(outside, jnp.max(jnp.where(allowed, scores, -1e30), axis=2))
    return peak, jnp.sum(jnp.where(allowed, jnp.exp(scores - peak[..., None]), 0.0), axis=2)


def joined_lse(outside, mine, other):
    peak = jnp.maximum(mine[0], other[0])
    total = mine[1] * jnp.exp(mine[0] - peak) + other[1] * jnp.exp(other[0] - peak)
    return peak + jnp.log(jnp.exp(outside - peak) + total)


def gathered(mine, u, v):
    partner = triple_swap(mine)
    own = (triple_shift(mine, 1), triple_shift(mine, 2))
    partner = jnp.where(u + v < 6, partner, mine)
    partner, *own = lax.optimization_barrier((partner,) + own)
    passed = (triple_shift(partner, 1), triple_shift(partner, 2))
    full = jnp.zeros((2, SEG, mine.shape[2]), BF)
    for half, pieces in ((u, (mine, *own)), (1 - u, (partner, *passed))):
        for steps, piece in enumerate(pieces):
            start = ((v + 3 - steps) % 3) * 128 + half * 64
            full = lax.dynamic_update_slice_in_dim(full, piece, start, 1)
    return full


def per_device(hidden, targets, padding, gold_logit, vocab_lse, cotangent):
    score_scale = 1.0 / math.sqrt(KW)
    core = lax.axis_index("dp") % 2
    r = lax.axis_index("tensor")
    u, v = r // 3, r % 3
    payload = with_codes(hidden, targets, padding)

    key_one = dp_permute(payload, first_keys())
    key_two = dp_permute(payload, second_keys())
    weight = cotangent * padding.astype(F32)
    row_data = jnp.stack([targets.astype(F32) + 1.0, gold_logit, vocab_lse, weight])
    row_data = rows_of(row_data, v * 128 + u * 64, 64, 1)
    row_data, late_payload = lax.optimization_barrier((row_data, payload))
    pair_hidden = core_swap(late_payload)[:SEG]
    row_data = jnp.stack([row_data, core_swap(row_data)])
    row_codes, gold, vocab, weight = (row_data[:, i] for i in range(4))

    key_own = jnp.where(core == 0, payload, key_one)
    key_own, key_two = lax.optimization_barrier((key_own, key_two))
    keys = [
        jnp.concatenate([key_one[:SEG], key_two[:SEG]], axis=0),
        jnp.concatenate([key_own[:SEG], key_two[:SEG]], axis=0),
    ]
    code_two = codes_of(key_two)
    codes = jnp.stack(
        [
            jnp.concatenate([codes_of(key_one), code_two]),
            jnp.concatenate([codes_of(key_own), code_two]),
        ]
    )

    def partial(queries, steps, half):
        start = ((v + steps) % 3) * 128 + half * 64
        parts = [partial_of(rows_of(q, start, 64), read) for q, read in zip(queries, keys)]
        return jnp.stack(parts)

    read_rows = [rows_of(hidden, ((v + steps) % 3) * 128 + (1 - u) * 64, 64) for steps in (1, 2)]
    own_sent = tuple(partial_of(rows, keys[0]) for rows in read_rows)
    *own_sent, pair_hidden = lax.optimization_barrier(own_sent + (pair_hidden,))
    sent = tuple(
        jnp.stack([mine, partial_of(rows_of(pair_hidden, start, 64), keys[1])])
        for mine, start in zip(own_sent, [((v + steps) % 3) * 128 + (1 - u) * 64 for steps in (1, 2)])
    )
    *sent, own, pair = lax.optimization_barrier(sent + (hidden, pair_hidden))
    queries = (own, pair)
    passing = partial(queries, 0, 1 - u) + triple_shift(sent[0], 1) + triple_shift(sent[1], 2)
    late = tuple(partial(queries, steps, u) for steps in (1, 2))
    passing, *late = lax.optimization_barrier((passing,) + late)
    from_partner = triple_swap(passing)
    scores = lax.optimization_barrier(partial(queries, 0, u) + from_partner)
    scores = (scores + triple_shift(late[0], 1) + triple_shift(late[1], 2)) * score_scale

    usable = jnp.broadcast_to((codes > 0.0)[:, None], scores.shape)
    matches = usable & (codes[:, None] == row_codes[:, :, None])
    total_part = summed_part(scores, usable, vocab)
    pos_part = summed_part(scores, matches, gold)
    stats = jnp.stack([*total_part, *pos_part], axis=1)
    other = core_swap(stats)
    other = jnp.concatenate([other[1:], other[:1]], axis=0)
    total_lse = joined_lse(vocab, total_part, (other[:, 0], other[:, 1]))
    pos_lse = joined_lse(gold, pos_part, (other[:, 2], other[:, 3]))
    spread = jnp.where(usable, jnp.exp(scores - total_lse[..., None]), 0.0) - jnp.where(
        matches, jnp.exp(scores - pos_lse[..., None]), 0.0
    )
    slopes = gathered((weight[..., None] * spread * score_scale).astype(BF), u, v)

    both_hidden = jnp.concatenate([hidden, pair_hidden], axis=0)
    flat = slopes.reshape(2 * SEG, 2 * SEG)
    pair_one = key_grad(slopes[1, :, :SEG], pair_hidden)
    grad_one = key_grad(slopes[0, :, :SEG], hidden) + jnp.where(core == 1, pair_one, 0.0)
    grad_one, flat = lax.optimization_barrier((grad_one.astype(BF), flat))
    home_one = dp_permute(grad_one, reverse(first_keys()))
    grad_two = key_grad(flat[:, SEG:], both_hidden).astype(BF)
    grad_two, flat = lax.optimization_barrier((grad_two, flat))
    home_two = dp_permute(grad_two, reverse(second_keys()))
    pair_grad = core_swap(jnp.dot(flat[SEG:], keys[1], preferred_element_type=F32).astype(BF))
    own_grad = jnp.dot(flat[:SEG], keys[0], preferred_element_type=F32)
    own_grad = lax.optimization_barrier(own_grad + jnp.where(core == 0, pair_one, 0.0))
    own_grad = lax.optimization_barrier(own_grad + home_one.astype(F32))
    own_grad = lax.optimization_barrier(own_grad + home_two.astype(F32))
    return (own_grad + pair_grad.astype(F32)).astype(BF)


def solution(mesh):
    placed = (P("dp", "tensor"), P("dp"), P("dp"), P("dp"), P("dp"), P("dp"))
    return jax.shard_map(
        per_device, mesh=mesh, in_specs=placed, out_specs=P("dp", "tensor"), check_vma=False
    )
```

```python
import math

import jax
import jax.numpy as jnp
from jax import lax
from jax.sharding import PartitionSpec as P

KW = 3840
SEG = 384
BF = jnp.bfloat16
F32 = jnp.float32


def dp_permute(value, pairs):
    return lax.ppermute(value, "dp", pairs)


def core_swap(value):
    return dp_permute(value, [(i, i ^ 1) for i in range(lax.axis_size("dp"))])


def key_pairs():
    count = lax.axis_size("dp")
    return [(i, (i + (4 if i % 2 == 0 else 2)) % count) for i in range(count)]


def reverse(pairs):
    return [(target, source) for source, target in pairs]


def triple_shift(value, steps):
    pairs = [(3 * u + v, 3 * u + (v + steps) % 3) for u in range(2) for v in range(3)]
    return lax.ppermute(value, "tensor", pairs)


def triple_swap(value):
    return lax.ppermute(value, "tensor", [(r, (r + 3) % 6) for r in range(6)])


def rows_of(value, start, size, axis=0):
    return lax.dynamic_slice_in_dim(value, start, size, axis)


def partial_of(queries, keys):
    return lax.dot_general(queries, keys, (((1,), (1,)), ((), ())), preferred_element_type=F32)


def key_grad(slopes, hidden):
    return lax.dot_general(slopes, hidden, (((0,), (0,)), ((), ())), preferred_element_type=F32)


def with_codes(hidden, targets, padding):
    code = jnp.where(padding == 1, targets + 1, 0)
    digits = jnp.stack([code >> 8, code & 255]).astype(BF)
    tail = jnp.pad(digits, ((0, 14), (0, hidden.shape[1] - SEG)))
    return jnp.concatenate([hidden, tail], axis=0)


def codes_of(payload):
    digits = lax.optimization_barrier(payload[SEG:])[:2, :SEG].astype(F32)
    return digits[0] * 256.0 + digits[1]


def summed_part(scores, allowed, outside):
    peak = jnp.maximum(outside, jnp.max(jnp.where(allowed, scores, -1e30), axis=2))
    return peak, jnp.sum(jnp.where(allowed, jnp.exp(scores - peak[..., None]), 0.0), axis=2)


def joined_lse(outside, mine, other):
    peak = jnp.maximum(mine[0], other[0])
    total = mine[1] * jnp.exp(mine[0] - peak) + other[1] * jnp.exp(other[0] - peak)
    return peak + jnp.log(jnp.exp(outside - peak) + total)


def gathered(mine, u, v):
    partner = triple_swap(mine)
    own = (triple_shift(mine, 1), triple_shift(mine, 2))
    partner = jnp.where(u + v < 6, partner, mine)
    partner, *own = lax.optimization_barrier((partner,) + own)
    passed = (triple_shift(partner, 1), triple_shift(partner, 2))
    full = jnp.zeros((2, SEG, mine.shape[2]), BF)
    for half, pieces in ((u, (mine, *own)), (1 - u, (partner, *passed))):
        for steps, piece in enumerate(pieces):
            start = ((v + 3 - steps) % 3) * 128 + half * 64
            full = lax.dynamic_update_slice_in_dim(full, piece, start, 1)
    return full


def per_device(hidden, targets, padding, gold_logit, vocab_lse, cotangent):
    score_scale = 1.0 / math.sqrt(KW)
    core = lax.axis_index("dp") % 2
    r = lax.axis_index("tensor")
    u, v = r // 3, r % 3
    payload = with_codes(hidden, targets, padding)

    pair_payload = core_swap(payload)
    pair_hidden = pair_payload[:SEG]
    both = dp_permute(jnp.concatenate([payload, pair_payload], axis=0), key_pairs())
    key_one, key_two = both[: SEG + 16], both[SEG + 16 :]
    weight = cotangent * padding.astype(F32)
    row_data = jnp.stack([targets.astype(F32) + 1.0, gold_logit, vocab_lse, weight])
    row_data = rows_of(row_data, v * 128 + u * 64, 64, 1)
    row_data = jnp.stack([row_data, core_swap(row_data)])
    row_codes, gold, vocab, weight = (row_data[:, i] for i in range(4))

    key_own = jnp.where(core == 0, payload, key_one)
    keys = [
        jnp.concatenate([key_one[:SEG], key_two[:SEG]], axis=0),
        jnp.concatenate([key_own[:SEG], key_two[:SEG]], axis=0),
    ]
    code_two = codes_of(key_two)
    codes = jnp.stack(
        [
            jnp.concatenate([codes_of(key_one), code_two]),
            jnp.concatenate([codes_of(key_own), code_two]),
        ]
    )

    def partial(queries, steps, half):
        start = ((v + steps) % 3) * 128 + half * 64
        parts = [partial_of(rows_of(q, start, 64), read) for q, read in zip(queries, keys)]
        return jnp.stack(parts)

    read_rows = [rows_of(hidden, ((v + steps) % 3) * 128 + (1 - u) * 64, 64) for steps in (1, 2)]
    own_sent = tuple(partial_of(rows, keys[0]) for rows in read_rows)
    *own_sent, pair_hidden = lax.optimization_barrier(own_sent + (pair_hidden,))
    sent = tuple(
        jnp.stack([mine, partial_of(rows_of(pair_hidden, start, 64), keys[1])])
        for mine, start in zip(own_sent, [((v + steps) % 3) * 128 + (1 - u) * 64 for steps in (1, 2)])
    )
    *sent, own, pair = lax.optimization_barrier(sent + (hidden, pair_hidden))
    queries = (own, pair)
    passing = partial(queries, 0, 1 - u) + triple_shift(sent[0], 1) + triple_shift(sent[1], 2)
    late = tuple(partial(queries, steps, u) for steps in (1, 2))
    passing, *late = lax.optimization_barrier((passing,) + late)
    from_partner = triple_swap(passing)
    scores = lax.optimization_barrier(partial(queries, 0, u) + from_partner)
    scores = (scores + triple_shift(late[0], 1) + triple_shift(late[1], 2)) * score_scale

    usable = jnp.broadcast_to((codes > 0.0)[:, None], scores.shape)
    matches = usable & (codes[:, None] == row_codes[:, :, None])
    total_part = summed_part(scores, usable, vocab)
    pos_part = summed_part(scores, matches, gold)
    stats = jnp.stack([*total_part, *pos_part], axis=1)
    other = core_swap(stats)
    other = jnp.concatenate([other[1:], other[:1]], axis=0)
    total_lse = joined_lse(vocab, total_part, (other[:, 0], other[:, 1]))
    pos_lse = joined_lse(gold, pos_part, (other[:, 2], other[:, 3]))
    spread = jnp.where(usable, jnp.exp(scores - total_lse[..., None]), 0.0) - jnp.where(
        matches, jnp.exp(scores - pos_lse[..., None]), 0.0
    )
    slopes = gathered((weight[..., None] * spread * score_scale).astype(BF), u, v)

    both_hidden = jnp.concatenate([hidden, pair_hidden], axis=0)
    flat = slopes.reshape(2 * SEG, 2 * SEG)
    grad_two = key_grad(flat[:, SEG:], both_hidden).astype(BF)
    grad_two, flat = lax.optimization_barrier((grad_two, flat))
    home_two = dp_permute(grad_two, reverse(key_pairs()))
    pair_one = key_grad(flat[SEG:, :SEG], pair_hidden)
    grad_one = key_grad(flat[:SEG, :SEG], hidden) + jnp.where(core == 1, pair_one, 0.0)
    grad_one, flat = lax.optimization_barrier((grad_one.astype(BF), flat))
    home_one = dp_permute(grad_one, reverse(key_pairs()))
    pair_grad = jnp.dot(flat[SEG:], keys[1], preferred_element_type=F32)
    pair_grad = lax.optimization_barrier(pair_grad) + home_two.astype(F32)
    pair_grad = core_swap(pair_grad.astype(BF))
    own_grad = jnp.dot(flat[:SEG], keys[0], preferred_element_type=F32)
    own_grad = lax.optimization_barrier(own_grad + jnp.where(core == 0, pair_one, 0.0))
    own_grad = lax.optimization_barrier(own_grad + home_one.astype(F32))
    return (own_grad + pair_grad.astype(F32)).astype(BF)


def solution(mesh):
    placed = (P("dp", "tensor"), P("dp"), P("dp"), P("dp"), P("dp"), P("dp"))
    return jax.shard_map(
        per_device, mesh=mesh, in_specs=placed, out_specs=P("dp", "tensor"), check_vma=False
    )
```

```python
import math

import jax
import jax.numpy as jnp
from jax import lax
from jax.sharding import PartitionSpec as P

KW = 3840
SEG = 384
BF = jnp.bfloat16
F32 = jnp.float32


def dp_permute(value, pairs):
    return lax.ppermute(value, "dp", pairs)


def core_swap(value):
    return dp_permute(value, [(i, i ^ 1) for i in range(lax.axis_size("dp"))])


def key_pairs():
    count = lax.axis_size("dp")
    return [(i, (i + (4 if i % 2 == 0 else 2)) % count) for i in range(count)]


def crossed_pairs():
    count = lax.axis_size("dp")
    return [(i, (i + 3) % count) for i in range(count)]


def reverse(pairs):
    return [(target, source) for source, target in pairs]


def triple_shift(value, steps):
    pairs = [(3 * u + v, 3 * u + (v + steps) % 3) for u in range(2) for v in range(3)]
    return lax.ppermute(value, "tensor", pairs)


def triple_swap(value):
    return lax.ppermute(value, "tensor", [(r, (r + 3) % 6) for r in range(6)])


def rows_of(value, start, size, axis=0):
    return lax.dynamic_slice_in_dim(value, start, size, axis)


def partial_of(queries, keys):
    return lax.dot_general(queries, keys, (((1,), (1,)), ((), ())), preferred_element_type=F32)


def key_grad(slopes, hidden):
    return lax.dot_general(slopes, hidden, (((0,), (0,)), ((), ())), preferred_element_type=F32)


def with_codes(hidden, targets, padding):
    code = jnp.where(padding == 1, targets + 1, 0)
    digits = jnp.stack([code >> 8, code & 255]).astype(BF)
    tail = jnp.pad(digits, ((0, 14), (0, hidden.shape[1] - SEG)))
    return jnp.concatenate([hidden, tail], axis=0)


def codes_of(payload):
    digits = lax.optimization_barrier(payload[SEG:])[:2, :SEG].astype(F32)
    return digits[0] * 256.0 + digits[1]


def summed_part(scores, allowed, outside):
    peak = jnp.maximum(outside, jnp.max(jnp.where(allowed, scores, -1e30), axis=2))
    return peak, jnp.sum(jnp.where(allowed, jnp.exp(scores - peak[..., None]), 0.0), axis=2)


def joined_lse(outside, mine, other):
    peak = jnp.maximum(mine[0], other[0])
    total = mine[1] * jnp.exp(mine[0] - peak) + other[1] * jnp.exp(other[0] - peak)
    return peak + jnp.log(jnp.exp(outside - peak) + total)


def gathered(mine, u, v):
    partner = triple_swap(mine)
    own = (triple_shift(mine, 1), triple_shift(mine, 2))
    partner = jnp.where(u + v < 6, partner, mine)
    partner, *own = lax.optimization_barrier((partner,) + own)
    passed = (triple_shift(partner, 1), triple_shift(partner, 2))
    full = jnp.zeros((2, SEG, mine.shape[2]), BF)
    for half, pieces in ((u, (mine, *own)), (1 - u, (partner, *passed))):
        for steps, piece in enumerate(pieces):
            start = ((v + 3 - steps) % 3) * 128 + half * 64
            full = lax.dynamic_update_slice_in_dim(full, piece, start, 1)
    return full


def per_device(hidden, targets, padding, gold_logit, vocab_lse, cotangent):
    score_scale = 1.0 / math.sqrt(KW)
    core = lax.axis_index("dp") % 2
    r = lax.axis_index("tensor")
    u, v = r // 3, r % 3
    payload = with_codes(hidden, targets, padding)

    key_one = dp_permute(payload, key_pairs())
    key_two = dp_permute(payload, crossed_pairs())
    weight = cotangent * padding.astype(F32)
    row_data = jnp.stack([targets.astype(F32) + 1.0, gold_logit, vocab_lse, weight])
    row_data = rows_of(row_data, v * 128 + u * 64, 64, 1)
    row_data, late_payload = lax.optimization_barrier((row_data, payload))
    pair_hidden = core_swap(late_payload)[:SEG]
    row_data = jnp.stack([row_data, core_swap(row_data)])
    row_codes, gold, vocab, weight = (row_data[:, i] for i in range(4))

    key_own = jnp.where(core == 0, payload, key_one)
    key_own, key_two = lax.optimization_barrier((key_own, key_two))
    keys = [
        jnp.concatenate([key_one[:SEG], key_two[:SEG]], axis=0),
        jnp.concatenate([key_own[:SEG], key_two[:SEG]], axis=0),
    ]
    code_two = codes_of(key_two)
    codes = jnp.stack(
        [
            jnp.concatenate([codes_of(key_one), code_two]),
            jnp.concatenate([codes_of(key_own), code_two]),
        ]
    )

    def partial(queries, steps, half):
        start = ((v + steps) % 3) * 128 + half * 64
        parts = [partial_of(rows_of(q, start, 64), read) for q, read in zip(queries, keys)]
        return jnp.stack(parts)

    read_rows = [rows_of(hidden, ((v + steps) % 3) * 128 + (1 - u) * 64, 64) for steps in (1, 2)]
    own_sent = tuple(partial_of(rows, keys[0]) for rows in read_rows)
    *own_sent, pair_hidden = lax.optimization_barrier(own_sent + (pair_hidden,))
    sent = tuple(
        jnp.stack([mine, partial_of(rows_of(pair_hidden, start, 64), keys[1])])
        for mine, start in zip(own_sent, [((v + steps) % 3) * 128 + (1 - u) * 64 for steps in (1, 2)])
    )
    *sent, own, pair = lax.optimization_barrier(sent + (hidden, pair_hidden))
    queries = (own, pair)
    passing = partial(queries, 0, 1 - u) + triple_shift(sent[0], 1) + triple_shift(sent[1], 2)
    late = tuple(partial(queries, steps, u) for steps in (1, 2))
    passing, *late = lax.optimization_barrier((passing,) + late)
    from_partner = triple_swap(passing)
    scores = lax.optimization_barrier(partial(queries, 0, u) + from_partner)
    scores = (scores + triple_shift(late[0], 1) + triple_shift(late[1], 2)) * score_scale

    usable = jnp.broadcast_to((codes > 0.0)[:, None], scores.shape)
    matches = usable & (codes[:, None] == row_codes[:, :, None])
    total_part = summed_part(scores, usable, vocab)
    pos_part = summed_part(scores, matches, gold)
    stats = jnp.stack([*total_part, *pos_part], axis=1)
    other = core_swap(stats)
    other = jnp.concatenate([other[1:], other[:1]], axis=0)
    total_lse = joined_lse(vocab, total_part, (other[:, 0], other[:, 1]))
    pos_lse = joined_lse(gold, pos_part, (other[:, 2], other[:, 3]))
    spread = jnp.where(usable, jnp.exp(scores - total_lse[..., None]), 0.0) - jnp.where(
        matches, jnp.exp(scores - pos_lse[..., None]), 0.0
    )
    slopes = gathered((weight[..., None] * spread * score_scale).astype(BF), u, v)

    both_hidden = jnp.concatenate([hidden, pair_hidden], axis=0)
    flat = slopes.reshape(2 * SEG, 2 * SEG)
    grad_two = key_grad(flat[:, SEG:], both_hidden).astype(BF)
    grad_two, flat = lax.optimization_barrier((grad_two, flat))
    home_two = dp_permute(grad_two, reverse(key_pairs()))
    pair_one = key_grad(flat[SEG:, :SEG], pair_hidden)
    grad_one = key_grad(flat[:SEG, :SEG], hidden) + jnp.where(core == 1, pair_one, 0.0)
    grad_one, flat = lax.optimization_barrier((grad_one.astype(BF), flat))
    home_one = dp_permute(grad_one, reverse(key_pairs()))
    pair_grad = jnp.dot(flat[SEG:], keys[1], preferred_element_type=F32)
    pair_grad = lax.optimization_barrier(pair_grad) + home_two.astype(F32)
    pair_grad = core_swap(pair_grad.astype(BF))
    own_grad = jnp.dot(flat[:SEG], keys[0], preferred_element_type=F32)
    own_grad = lax.optimization_barrier(own_grad + jnp.where(core == 0, pair_one, 0.0))
    own_grad = lax.optimization_barrier(own_grad + home_one.astype(F32))
    return (own_grad + pair_grad.astype(F32)).astype(BF)


def solution(mesh):
    placed = (P("dp", "tensor"), P("dp"), P("dp"), P("dp"), P("dp"), P("dp"))
    return jax.shard_map(
        per_device, mesh=mesh, in_specs=placed, out_specs=P("dp", "tensor"), check_vma=False
    )
```

```python
import math

import jax
import jax.numpy as jnp
from jax import lax
from jax.sharding import PartitionSpec as P

KW = 3840
SEG = 384
BF = jnp.bfloat16
F32 = jnp.float32


def dp_permute(value, pairs):
    return lax.ppermute(value, "dp", pairs)


def core_swap(value):
    return dp_permute(value, [(i, i ^ 1) for i in range(lax.axis_size("dp"))])


def key_pairs():
    count = lax.axis_size("dp")
    return [(i, (i + (4 if i % 2 == 0 else 2)) % count) for i in range(count)]


def crossed_pairs():
    count = lax.axis_size("dp")
    return [(i, (i + 3) % count) for i in range(count)]


def reverse(pairs):
    return [(target, source) for source, target in pairs]


def triple(steps):
    return lambda r: 3 * (r // 3) + (r + steps) % 3


def stride(steps):
    return lambda r: (r + 2 * steps) % 6


def across(r):
    return (r + 3) % 6


def beside(r):
    return r + 1 - 2 * (r % 2)


def line_permute(value, even_to, odd_to):
    size = lax.axis_size("tensor")
    pairs = [
        (i * size + r, i * size + (odd_to if i % 2 else even_to)(r))
        for i in range(lax.axis_size("dp"))
        for r in range(size)
    ]
    return lax.ppermute(value, ("dp", "tensor"), pairs)


def row_start(device):
    return (device % 3) * 128 + (device // 3) * 64


def rows_of(value, start, size, axis=0):
    return lax.dynamic_slice_in_dim(value, start, size, axis)


def partial_of(queries, keys):
    return lax.dot_general(queries, keys, (((1,), (1,)), ((), ())), preferred_element_type=F32)


def key_grad(slopes, hidden):
    return lax.dot_general(slopes, hidden, (((0,), (0,)), ((), ())), preferred_element_type=F32)


def with_codes(hidden, targets, padding):
    code = jnp.where(padding == 1, targets + 1, 0)
    digits = jnp.stack([code >> 8, code & 255]).astype(BF)
    tail = jnp.pad(digits, ((0, 14), (0, hidden.shape[1] - SEG)))
    return jnp.concatenate([hidden, tail], axis=0)


def codes_of(payload):
    digits = lax.optimization_barrier(payload[SEG:])[:2, :SEG].astype(F32)
    return digits[0] * 256.0 + digits[1]


def summed_part(scores, allowed, outside):
    peak = jnp.maximum(outside, jnp.max(jnp.where(allowed, scores, -1e30), axis=2))
    return peak, jnp.sum(jnp.where(allowed, jnp.exp(scores - peak[..., None]), 0.0), axis=2)


def joined_lse(outside, mine, other):
    peak = jnp.maximum(mine[0], other[0])
    total = mine[1] * jnp.exp(mine[0] - peak) + other[1] * jnp.exp(other[0] - peak)
    return peak + jnp.log(jnp.exp(outside - peak) + total)


def gathered(mine, core, r):
    def owner(even, odd):
        return jnp.where(core == 0, even(r), odd(r))

    paired = line_permute(mine, beside, across)
    one = line_permute(mine, stride(1), triple(1))
    two = line_permute(mine, stride(2), triple(2))
    passed_one = line_permute(jnp.where(core == 0, one, paired), beside, triple(1))
    passed_two = line_permute(jnp.where(core == 0, two, paired), beside, triple(2))
    pieces = (
        (mine, r),
        (paired, owner(beside, across)),
        (one, owner(stride(2), triple(2))),
        (two, owner(stride(1), triple(1))),
        (passed_one, owner(lambda q: beside(stride(2)(q)), lambda q: across(triple(2)(q)))),
        (passed_two, owner(lambda q: beside(stride(1)(q)), lambda q: across(triple(1)(q)))),
    )
    full = jnp.zeros((2, SEG, mine.shape[2]), BF)
    for piece, device in pieces:
        full = lax.dynamic_update_slice_in_dim(full, piece, row_start(device), 1)
    return full


def per_device(hidden, targets, padding, gold_logit, vocab_lse, cotangent):
    score_scale = 1.0 / math.sqrt(KW)
    core = lax.axis_index("dp") % 2
    r = lax.axis_index("tensor")
    payload = with_codes(hidden, targets, padding)

    key_one = dp_permute(payload, key_pairs())
    key_two = dp_permute(payload, crossed_pairs())
    weight = cotangent * padding.astype(F32)
    row_data = jnp.stack([targets.astype(F32) + 1.0, gold_logit, vocab_lse, weight])
    row_data = rows_of(row_data, row_start(r), 64, 1)
    row_data, late_payload = lax.optimization_barrier((row_data, payload))
    pair_hidden = core_swap(late_payload)[:SEG]
    row_data = jnp.stack([row_data, core_swap(row_data)])
    row_codes, gold, vocab, weight = (row_data[:, i] for i in range(4))

    key_own = jnp.where(core == 0, payload, key_one)
    key_own, key_two = lax.optimization_barrier((key_own, key_two))
    keys = [
        jnp.concatenate([key_one[:SEG], key_two[:SEG]], axis=0),
        jnp.concatenate([key_own[:SEG], key_two[:SEG]], axis=0),
    ]
    code_two = codes_of(key_two)
    codes = jnp.stack(
        [
            jnp.concatenate([codes_of(key_one), code_two]),
            jnp.concatenate([codes_of(key_own), code_two]),
        ]
    )

    def owner(even, odd):
        return jnp.where(core == 0, even(r), odd(r))

    def partial(queries, device):
        parts = [
            partial_of(rows_of(q, row_start(device), 64), read) for q, read in zip(queries, keys)
        ]
        return jnp.stack(parts)

    ahead = [
        owner(lambda q: beside(stride(1)(q)), lambda q: across(triple(1)(q))),
        owner(lambda q: beside(stride(2)(q)), lambda q: across(triple(2)(q))),
    ]
    own_sent = tuple(partial_of(rows_of(hidden, row_start(d), 64), keys[0]) for d in ahead)
    *own_sent, pair_hidden = lax.optimization_barrier(own_sent + (pair_hidden,))
    sent = tuple(
        jnp.stack([mine, partial_of(rows_of(pair_hidden, row_start(d), 64), keys[1])])
        for mine, d in zip(own_sent, ahead)
    )
    *sent, own, pair = lax.optimization_barrier(sent + (hidden, pair_hidden))
    queries = (own, pair)
    in_one = line_permute(sent[0], beside, triple(1))
    in_two = line_permute(sent[1], beside, triple(2))
    paired = partial(queries, owner(beside, across)) + jnp.where(core == 1, in_one + in_two, 0.0)
    one = partial(queries, owner(stride(1), triple(1))) + jnp.where(core == 0, in_one, 0.0)
    two = partial(queries, owner(stride(2), triple(2))) + jnp.where(core == 0, in_two, 0.0)
    paired, one, two = lax.optimization_barrier((paired, one, two))
    paired = line_permute(paired, beside, across)
    scores = lax.optimization_barrier(partial(queries, r) + paired)
    one = line_permute(one, stride(1), triple(1))
    two = line_permute(two, stride(2), triple(2))
    scores = (scores + one + two) * score_scale

    usable = jnp.broadcast_to((codes > 0.0)[:, None], scores.shape)
    matches = usable & (codes[:, None] == row_codes[:, :, None])
    total_part = summed_part(scores, usable, vocab)
    pos_part = summed_part(scores, matches, gold)
    stats = jnp.stack([*total_part, *pos_part], axis=1)
    other = core_swap(stats)
    other = jnp.concatenate([other[1:], other[:1]], axis=0)
    total_lse = joined_lse(vocab, total_part, (other[:, 0], other[:, 1]))
    pos_lse = joined_lse(gold, pos_part, (other[:, 2], other[:, 3]))
    spread = jnp.where(usable, jnp.exp(scores - total_lse[..., None]), 0.0) - jnp.where(
        matches, jnp.exp(scores - pos_lse[..., None]), 0.0
    )
    slopes = gathered((weight[..., None] * spread * score_scale).astype(BF), core, r)

    both_hidden = jnp.concatenate([hidden, pair_hidden], axis=0)
    flat = slopes.reshape(2 * SEG, 2 * SEG)
    grad_two = key_grad(flat[:, SEG:], both_hidden).astype(BF)
    grad_two, flat = lax.optimization_barrier((grad_two, flat))
    home_two = dp_permute(grad_two, reverse(key_pairs()))
    pair_one = key_grad(flat[SEG:, :SEG], pair_hidden)
    grad_one = key_grad(flat[:SEG, :SEG], hidden) + jnp.where(core == 1, pair_one, 0.0)
    grad_one, flat = lax.optimization_barrier((grad_one.astype(BF), flat))
    home_one = dp_permute(grad_one, reverse(key_pairs()))
    pair_grad = jnp.dot(flat[SEG:], keys[1], preferred_element_type=F32)
    pair_grad = lax.optimization_barrier(pair_grad) + home_two.astype(F32)
    pair_grad = core_swap(pair_grad.astype(BF))
    own_grad = jnp.dot(flat[:SEG], keys[0], preferred_element_type=F32)
    own_grad = lax.optimization_barrier(own_grad + jnp.where(core == 0, pair_one, 0.0))
    own_grad = lax.optimization_barrier(own_grad + home_one.astype(F32))
    return (own_grad + pair_grad.astype(F32)).astype(BF)


def solution(mesh):
    placed = (P("dp", "tensor"), P("dp"), P("dp"), P("dp"), P("dp"), P("dp"))
    return jax.shard_map(
        per_device, mesh=mesh, in_specs=placed, out_specs=P("dp", "tensor"), check_vma=False
    )
```

```python
import math

import jax
import jax.numpy as jnp
from jax import lax
from jax.sharding import PartitionSpec as P

KW = 3840
SEG = 384
BF = jnp.bfloat16
F32 = jnp.float32


def dp_permute(value, pairs):
    return lax.ppermute(value, "dp", pairs)


def core_swap(value):
    return dp_permute(value, [(i, i ^ 1) for i in range(lax.axis_size("dp"))])


def key_pairs():
    count = lax.axis_size("dp")
    return [(i, (i + (4 if i % 2 == 0 else 2)) % count) for i in range(count)]


def crossed_pairs():
    count = lax.axis_size("dp")
    return [(i, (i + 3) % count) for i in range(count)]


def reverse(pairs):
    return [(target, source) for source, target in pairs]


def triple(steps):
    return lambda r: 3 * (r // 3) + (r + steps) % 3


def stride(steps):
    return lambda r: (r + 2 * steps) % 6


def across(r):
    return (r + 3) % 6


def beside(r):
    return r + 1 - 2 * (r % 2)


def line_permute(value, even_to, odd_to):
    size = lax.axis_size("tensor")
    pairs = [
        (i * size + r, i * size + (odd_to if i % 2 else even_to)(r))
        for i in range(lax.axis_size("dp"))
        for r in range(size)
    ]
    return lax.ppermute(value, ("dp", "tensor"), pairs)


def row_start(device):
    return (device % 3) * 128 + (device // 3) * 64


def rows_of(value, start, size, axis=0):
    return lax.dynamic_slice_in_dim(value, start, size, axis)


def partial_of(queries, keys):
    return lax.dot_general(queries, keys, (((1,), (1,)), ((), ())), preferred_element_type=F32)


def key_grad(slopes, hidden):
    return lax.dot_general(slopes, hidden, (((0,), (0,)), ((), ())), preferred_element_type=F32)


def with_codes(hidden, targets, padding):
    code = jnp.where(padding == 1, targets + 1, 0)
    digits = jnp.stack([code >> 8, code & 255]).astype(BF)
    tail = jnp.pad(digits, ((0, 14), (0, hidden.shape[1] - SEG)))
    return jnp.concatenate([hidden, tail], axis=0)


def codes_of(payload):
    digits = lax.optimization_barrier(payload[SEG:])[:2, :SEG].astype(F32)
    return digits[0] * 256.0 + digits[1]


def summed_part(scores, allowed, outside):
    peak = jnp.maximum(outside, jnp.max(jnp.where(allowed, scores, -1e30), axis=2))
    return peak, jnp.sum(jnp.where(allowed, jnp.exp(scores - peak[..., None]), 0.0), axis=2)


def joined_lse(outside, mine, other):
    peak = jnp.maximum(mine[0], other[0])
    total = mine[1] * jnp.exp(mine[0] - peak) + other[1] * jnp.exp(other[0] - peak)
    return peak + jnp.log(jnp.exp(outside - peak) + total)


def gathered(mine, core, r):
    def owner(even, odd):
        return jnp.where(core == 0, even(r), odd(r))

    paired = line_permute(mine, beside, across)
    one = line_permute(mine, stride(1), triple(1))
    two = line_permute(mine, stride(2), triple(2))
    passed_one = line_permute(jnp.where(core == 0, one, paired), beside, triple(1))
    passed_two = line_permute(jnp.where(core == 0, two, paired), beside, triple(2))
    pieces = (
        (mine, r),
        (paired, owner(beside, across)),
        (one, owner(stride(2), triple(2))),
        (two, owner(stride(1), triple(1))),
        (passed_one, owner(lambda q: beside(stride(2)(q)), lambda q: across(triple(2)(q)))),
        (passed_two, owner(lambda q: beside(stride(1)(q)), lambda q: across(triple(1)(q)))),
    )
    full = jnp.zeros((2, SEG, mine.shape[2]), BF)
    for piece, device in pieces:
        full = lax.dynamic_update_slice_in_dim(full, piece, row_start(device), 1)
    return full


def per_device(hidden, targets, padding, gold_logit, vocab_lse, cotangent):
    score_scale = 1.0 / math.sqrt(KW)
    core = lax.axis_index("dp") % 2
    r = lax.axis_index("tensor")
    payload = with_codes(hidden, targets, padding)

    key_one = dp_permute(payload, key_pairs())
    key_two = dp_permute(payload, crossed_pairs())
    weight = cotangent * padding.astype(F32)
    row_data = jnp.stack([targets.astype(F32) + 1.0, gold_logit, vocab_lse, weight])
    row_data = rows_of(row_data, row_start(r), 64, 1)
    row_data, late_payload = lax.optimization_barrier((row_data, payload))
    pair_hidden = core_swap(late_payload)[:SEG]
    row_data = jnp.stack([row_data, core_swap(row_data)])
    row_codes, gold, vocab, weight = (row_data[:, i] for i in range(4))

    key_own = jnp.where(core == 0, payload, key_one)
    key_own, key_two = lax.optimization_barrier((key_own, key_two))
    keys = [
        jnp.concatenate([key_one[:SEG], key_two[:SEG]], axis=0),
        jnp.concatenate([key_own[:SEG], key_two[:SEG]], axis=0),
    ]
    code_two = codes_of(key_two)
    codes = jnp.stack(
        [
            jnp.concatenate([codes_of(key_one), code_two]),
            jnp.concatenate([codes_of(key_own), code_two]),
        ]
    )

    def owner(even, odd):
        return jnp.where(core == 0, even(r), odd(r))

    own_part = partial_of(hidden, keys[0])
    own_part, pair_hidden = lax.optimization_barrier((own_part, pair_hidden))
    pair_part = partial_of(pair_hidden, keys[1])

    def partial(device):
        start = row_start(device)
        return jnp.stack([rows_of(own_part, start, 64), rows_of(pair_part, start, 64)])

    ahead_one = partial(owner(lambda q: beside(stride(1)(q)), lambda q: across(triple(1)(q))))
    ahead_two = partial(owner(lambda q: beside(stride(2)(q)), lambda q: across(triple(2)(q))))
    in_one = line_permute(ahead_one, beside, triple(1))
    in_two = line_permute(ahead_two, beside, triple(2))
    paired = partial(owner(beside, across)) + jnp.where(core == 1, in_one + in_two, 0.0)
    one = partial(owner(stride(1), triple(1))) + jnp.where(core == 0, in_one, 0.0)
    two = partial(owner(stride(2), triple(2))) + jnp.where(core == 0, in_two, 0.0)
    paired, one, two = lax.optimization_barrier((paired, one, two))
    paired = line_permute(paired, beside, across)
    scores = lax.optimization_barrier(partial(r) + paired)
    one = line_permute(one, stride(1), triple(1))
    two = line_permute(two, stride(2), triple(2))
    scores = (scores + one + two) * score_scale

    usable = jnp.broadcast_to((codes > 0.0)[:, None], scores.shape)
    matches = usable & (codes[:, None] == row_codes[:, :, None])
    total_part = summed_part(scores, usable, vocab)
    pos_part = summed_part(scores, matches, gold)
    stats = jnp.stack([*total_part, *pos_part], axis=1)
    other = core_swap(stats)
    other = jnp.concatenate([other[1:], other[:1]], axis=0)
    total_lse = joined_lse(vocab, total_part, (other[:, 0], other[:, 1]))
    pos_lse = joined_lse(gold, pos_part, (other[:, 2], other[:, 3]))
    spread = jnp.where(usable, jnp.exp(scores - total_lse[..., None]), 0.0) - jnp.where(
        matches, jnp.exp(scores - pos_lse[..., None]), 0.0
    )
    slopes = gathered((weight[..., None] * spread * score_scale).astype(BF), core, r)

    both_hidden = jnp.concatenate([hidden, pair_hidden], axis=0)
    flat = slopes.reshape(2 * SEG, 2 * SEG)
    grad_two = key_grad(flat[:, SEG:], both_hidden).astype(BF)
    grad_two, flat = lax.optimization_barrier((grad_two, flat))
    home_two = dp_permute(grad_two, reverse(key_pairs()))
    pair_one = key_grad(flat[SEG:, :SEG], pair_hidden)
    grad_one = key_grad(flat[:SEG, :SEG], hidden) + jnp.where(core == 1, pair_one, 0.0)
    grad_one, flat = lax.optimization_barrier((grad_one.astype(BF), flat))
    home_one = dp_permute(grad_one, reverse(key_pairs()))
    pair_grad = jnp.dot(flat[SEG:], keys[1], preferred_element_type=F32)
    pair_grad = lax.optimization_barrier(pair_grad) + home_two.astype(F32)
    pair_grad = core_swap(pair_grad.astype(BF))
    own_grad = jnp.dot(flat[:SEG], keys[0], preferred_element_type=F32)
    own_grad = lax.optimization_barrier(own_grad + jnp.where(core == 0, pair_one, 0.0))
    own_grad = lax.optimization_barrier(own_grad + home_one.astype(F32))
    return (own_grad + pair_grad.astype(F32)).astype(BF)


def solution(mesh):
    placed = (P("dp", "tensor"), P("dp"), P("dp"), P("dp"), P("dp"), P("dp"))
    return jax.shard_map(
        per_device, mesh=mesh, in_specs=placed, out_specs=P("dp", "tensor"), check_vma=False
    )
```

```python
import math

import jax
import jax.numpy as jnp
from jax import lax
from jax.sharding import PartitionSpec as P

KW = 3840
SEG = 384
BF = jnp.bfloat16
F32 = jnp.float32


def dp_permute(value, pairs):
    return lax.ppermute(value, "dp", pairs)


def core_swap(value):
    return dp_permute(value, [(i, i ^ 1) for i in range(lax.axis_size("dp"))])


def key_pairs():
    count = lax.axis_size("dp")
    return [(i, (i + (4 if i % 2 == 0 else 2)) % count) for i in range(count)]


def crossed_pairs():
    count = lax.axis_size("dp")
    return [(i, (i + 3) % count) for i in range(count)]


def reverse(pairs):
    return [(target, source) for source, target in pairs]


def triple(steps):
    return lambda r: 3 * (r // 3) + (r + steps) % 3


def stride(steps):
    return lambda r: (r + 2 * steps) % 6


def across(r):
    return (r + 3) % 6


def beside(r):
    return r + 1 - 2 * (r % 2)


def line_permute(value, even_to, odd_to):
    size = lax.axis_size("tensor")
    pairs = [
        (i * size + r, i * size + (odd_to if i % 2 else even_to)(r))
        for i in range(lax.axis_size("dp"))
        for r in range(size)
    ]
    return lax.ppermute(value, ("dp", "tensor"), pairs)


def row_start(device):
    return (device % 3) * 128 + (device // 3) * 64


def rows_of(value, start, size, axis=0):
    return lax.dynamic_slice_in_dim(value, start, size, axis)


def partial_of(queries, keys):
    return lax.dot_general(queries, keys, (((1,), (1,)), ((), ())), preferred_element_type=F32)


def key_grad(slopes, hidden):
    return lax.dot_general(slopes, hidden, (((0,), (0,)), ((), ())), preferred_element_type=F32)


def with_codes(hidden, targets, padding):
    code = jnp.where(padding == 1, targets + 1, 0)
    digits = jnp.stack([code >> 8, code & 255]).astype(BF)
    tail = jnp.pad(digits, ((0, 14), (0, hidden.shape[1] - SEG)))
    return jnp.concatenate([hidden, tail], axis=0)


def codes_of(payload):
    digits = lax.optimization_barrier(payload[SEG:])[:2, :SEG].astype(F32)
    return digits[0] * 256.0 + digits[1]


def summed_part(scores, allowed, outside):
    peak = jnp.maximum(outside, jnp.max(jnp.where(allowed, scores, -1e30), axis=2))
    return peak, jnp.sum(jnp.where(allowed, jnp.exp(scores - peak[..., None]), 0.0), axis=2)


def joined_lse(outside, mine, other):
    peak = jnp.maximum(mine[0], other[0])
    total = mine[1] * jnp.exp(mine[0] - peak) + other[1] * jnp.exp(other[0] - peak)
    return peak + jnp.log(jnp.exp(outside - peak) + total)


def gathered(mine, core, r):
    def owner(even, odd):
        return jnp.where(core == 0, even(r), odd(r))

    paired = line_permute(mine, beside, across)
    one = line_permute(mine, stride(1), triple(1))
    two = line_permute(mine, stride(2), triple(2))
    passed_one = line_permute(jnp.where(core == 0, one, paired), beside, triple(1))
    passed_two = line_permute(jnp.where(core == 0, two, paired), beside, triple(2))
    pieces = (
        (mine, r),
        (paired, owner(beside, across)),
        (one, owner(stride(2), triple(2))),
        (two, owner(stride(1), triple(1))),
        (passed_one, owner(lambda q: beside(stride(2)(q)), lambda q: across(triple(2)(q)))),
        (passed_two, owner(lambda q: beside(stride(1)(q)), lambda q: across(triple(1)(q)))),
    )
    full = jnp.zeros((2, SEG, mine.shape[2]), BF)
    for piece, device in pieces:
        full = lax.dynamic_update_slice_in_dim(full, piece, row_start(device), 1)
    return full


def per_device(hidden, targets, padding, gold_logit, vocab_lse, cotangent):
    score_scale = 1.0 / math.sqrt(KW)
    core = lax.axis_index("dp") % 2
    r = lax.axis_index("tensor")
    payload = with_codes(hidden, targets, padding)

    key_one = dp_permute(payload, key_pairs())
    key_two = dp_permute(payload, crossed_pairs())
    weight = cotangent * padding.astype(F32)
    row_data = jnp.stack([targets.astype(F32) + 1.0, gold_logit, vocab_lse, weight])
    row_data = rows_of(row_data, row_start(r), 64, 1)
    row_data, late_payload = lax.optimization_barrier((row_data, payload))
    pair_hidden = core_swap(late_payload)[:SEG]
    row_data = jnp.stack([row_data, core_swap(row_data)])
    row_codes, gold, vocab, weight = (row_data[:, i] for i in range(4))

    key_own = jnp.where(core == 0, payload, key_one)
    key_own, key_two = lax.optimization_barrier((key_own, key_two))
    keys = [
        jnp.concatenate([key_one[:SEG], key_two[:SEG]], axis=0),
        jnp.concatenate([key_own[:SEG], key_two[:SEG]], axis=0),
    ]
    code_two = codes_of(key_two)
    codes = jnp.stack(
        [
            jnp.concatenate([codes_of(key_one), code_two]),
            jnp.concatenate([codes_of(key_own), code_two]),
        ]
    )

    def owner(even, odd):
        return jnp.where(core == 0, even(r), odd(r))

    def products(queries, read, one, two):
        rows = [rows_of(queries, row_start(device), 64) for device in (one, two)]
        return partial_of(jnp.concatenate(rows, axis=0), read)

    def blocks(own, pair):
        return jnp.stack([own[:64], pair[:64]]), jnp.stack([own[64:], pair[64:]])

    ahead = [
        owner(lambda q: beside(stride(1)(q)), lambda q: across(triple(1)(q))),
        owner(lambda q: beside(stride(2)(q)), lambda q: across(triple(2)(q))),
    ]
    own = payload[:SEG]
    own_sent = products(own, keys[0], *ahead)
    own_sent, pair_hidden = lax.optimization_barrier((own_sent, pair_hidden))
    sent = blocks(own_sent, products(pair_hidden, keys[1], *ahead))
    *sent, own, pair = lax.optimization_barrier(sent + (own, pair_hidden))
    in_one = line_permute(sent[0], beside, triple(1))
    in_two = line_permute(sent[1], beside, triple(2))
    ends = (owner(stride(1), triple(1)), owner(stride(2), triple(2)))
    one, two = blocks(products(own, keys[0], *ends), products(pair, keys[1], *ends))
    ends = (owner(beside, across), r)
    paired, kept = blocks(products(own, keys[0], *ends), products(pair, keys[1], *ends))
    paired = paired + jnp.where(core == 1, in_one + in_two, 0.0)
    one = one + jnp.where(core == 0, in_one, 0.0)
    two = two + jnp.where(core == 0, in_two, 0.0)
    paired, one, two = lax.optimization_barrier((paired, one, two))
    paired = line_permute(paired, beside, across)
    scores = lax.optimization_barrier(kept + paired)
    one = line_permute(one, stride(1), triple(1))
    two = line_permute(two, stride(2), triple(2))
    scores = (scores + one + two) * score_scale

    usable = jnp.broadcast_to((codes > 0.0)[:, None], scores.shape)
    matches = usable & (codes[:, None] == row_codes[:, :, None])
    total_part = summed_part(scores, usable, vocab)
    pos_part = summed_part(scores, matches, gold)
    stats = jnp.stack([*total_part, *pos_part], axis=1)
    other = core_swap(stats)
    other = jnp.concatenate([other[1:], other[:1]], axis=0)
    total_lse = joined_lse(vocab, total_part, (other[:, 0], other[:, 1]))
    pos_lse = joined_lse(gold, pos_part, (other[:, 2], other[:, 3]))
    spread = jnp.where(usable, jnp.exp(scores - total_lse[..., None]), 0.0) - jnp.where(
        matches, jnp.exp(scores - pos_lse[..., None]), 0.0
    )
    slopes = gathered((weight[..., None] * spread * score_scale).astype(BF), core, r)

    both_hidden = jnp.concatenate([hidden, pair_hidden], axis=0)
    flat = slopes.reshape(2 * SEG, 2 * SEG)
    grad_two = key_grad(flat[:, SEG:], both_hidden).astype(BF)
    grad_two, flat = lax.optimization_barrier((grad_two, flat))
    home_two = dp_permute(grad_two, reverse(key_pairs()))
    pair_one = key_grad(flat[SEG:, :SEG], pair_hidden)
    grad_one = key_grad(flat[:SEG, :SEG], hidden) + jnp.where(core == 1, pair_one, 0.0)
    grad_one, flat = lax.optimization_barrier((grad_one.astype(BF), flat))
    home_one = dp_permute(grad_one, reverse(key_pairs()))
    pair_grad = jnp.dot(flat[SEG:], keys[1], preferred_element_type=F32)
    pair_grad = lax.optimization_barrier(pair_grad) + home_two.astype(F32)
    pair_grad = core_swap(pair_grad.astype(BF))
    own_grad = jnp.dot(flat[:SEG], keys[0], preferred_element_type=F32)
    own_grad = lax.optimization_barrier(own_grad + jnp.where(core == 0, pair_one, 0.0))
    own_grad = lax.optimization_barrier(own_grad + home_one.astype(F32))
    return (own_grad + pair_grad.astype(F32)).astype(BF)


def solution(mesh):
    placed = (P("dp", "tensor"), P("dp"), P("dp"), P("dp"), P("dp"), P("dp"))
    return jax.shard_map(
        per_device, mesh=mesh, in_specs=placed, out_specs=P("dp", "tensor"), check_vma=False
    )
```

```python
import math

import jax
import jax.numpy as jnp
from jax import lax
from jax.sharding import PartitionSpec as P

KW = 3840
SEG = 384
BF = jnp.bfloat16
F32 = jnp.float32


def dp_permute(value, pairs):
    return lax.ppermute(value, "dp", pairs)


def core_swap(value):
    return dp_permute(value, [(i, i ^ 1) for i in range(lax.axis_size("dp"))])


def key_pairs():
    count = lax.axis_size("dp")
    return [(i, (i + (4 if i % 2 == 0 else 2)) % count) for i in range(count)]


def crossed_pairs():
    count = lax.axis_size("dp")
    return [(i, (i + 3) % count) for i in range(count)]


def reverse(pairs):
    return [(target, source) for source, target in pairs]


def triple(steps):
    return lambda r: 3 * (r // 3) + (r + steps) % 3


def stride(steps):
    return lambda r: (r + 2 * steps) % 6


def across(r):
    return (r + 3) % 6


def beside(r):
    return r + 1 - 2 * (r % 2)


def line_permute(value, even_to, odd_to):
    size = lax.axis_size("tensor")
    pairs = [
        (i * size + r, i * size + (odd_to if i % 2 else even_to)(r))
        for i in range(lax.axis_size("dp"))
        for r in range(size)
    ]
    return lax.ppermute(value, ("dp", "tensor"), pairs)


def row_start(device):
    return (device % 3) * 128 + (device // 3) * 64


def rows_of(value, start, size, axis=0):
    return lax.dynamic_slice_in_dim(value, start, size, axis)


def partial_of(queries, keys):
    return lax.dot_general(queries, keys, (((1,), (1,)), ((), ())), preferred_element_type=F32)


def key_grad(slopes, hidden):
    return lax.dot_general(slopes, hidden, (((0,), (0,)), ((), ())), preferred_element_type=F32)


def with_codes(hidden, targets, padding):
    code = jnp.where(padding == 1, targets + 1, 0)
    digits = jnp.stack([code >> 8, code & 255]).astype(BF)
    tail = jnp.pad(digits, ((0, 14), (0, hidden.shape[1] - SEG)))
    return jnp.concatenate([hidden, tail], axis=0)


def codes_of(payload):
    digits = lax.optimization_barrier(payload[SEG:])[:2, :SEG].astype(F32)
    return digits[0] * 256.0 + digits[1]


def summed_part(scores, allowed, outside):
    peak = jnp.maximum(outside, jnp.max(jnp.where(allowed, scores, -1e30), axis=2))
    return peak, jnp.sum(jnp.where(allowed, jnp.exp(scores - peak[..., None]), 0.0), axis=2)


def joined_lse(outside, mine, other):
    peak = jnp.maximum(mine[0], other[0])
    total = mine[1] * jnp.exp(mine[0] - peak) + other[1] * jnp.exp(other[0] - peak)
    return peak + jnp.log(jnp.exp(outside - peak) + total)


def gathered(mine, core, r):
    def owner(even, odd):
        return jnp.where(core == 0, even(r), odd(r))

    paired = line_permute(mine, beside, across)
    one = line_permute(mine, stride(1), triple(1))
    two = line_permute(mine, stride(2), triple(2))
    passed_one = line_permute(jnp.where(core == 0, one, paired), beside, triple(1))
    passed_two = line_permute(jnp.where(core == 0, two, paired), beside, triple(2))
    pieces = (
        (mine, r),
        (paired, owner(beside, across)),
        (one, owner(stride(2), triple(2))),
        (two, owner(stride(1), triple(1))),
        (passed_one, owner(lambda q: beside(stride(2)(q)), lambda q: across(triple(2)(q)))),
        (passed_two, owner(lambda q: beside(stride(1)(q)), lambda q: across(triple(1)(q)))),
    )
    full = jnp.zeros((2, SEG, mine.shape[2]), BF)
    for piece, device in pieces:
        full = lax.dynamic_update_slice_in_dim(full, piece, row_start(device), 1)
    return full


def per_device(hidden, targets, padding, gold_logit, vocab_lse, cotangent):
    score_scale = 1.0 / math.sqrt(KW)
    core = lax.axis_index("dp") % 2
    r = lax.axis_index("tensor")
    payload = lax.optimization_barrier(with_codes(hidden, targets, padding))

    key_one = dp_permute(payload, key_pairs())
    key_two = dp_permute(payload, crossed_pairs())
    weight = cotangent * padding.astype(F32)
    row_data = jnp.stack([targets.astype(F32) + 1.0, gold_logit, vocab_lse, weight])
    row_data = rows_of(row_data, row_start(r), 64, 1)
    row_data, late_payload = lax.optimization_barrier((row_data, payload))
    pair_hidden = core_swap(late_payload)[:SEG]
    row_data = jnp.stack([row_data, core_swap(row_data)])
    row_codes, gold, vocab, weight = (row_data[:, i] for i in range(4))

    key_own = jnp.where(core == 0, payload, key_one)
    key_own, key_two = lax.optimization_barrier((key_own, key_two))
    keys = [
        jnp.concatenate([key_one[:SEG], key_two[:SEG]], axis=0),
        jnp.concatenate([key_own[:SEG], key_two[:SEG]], axis=0),
    ]
    code_two = codes_of(key_two)
    codes = jnp.stack(
        [
            jnp.concatenate([codes_of(key_one), code_two]),
            jnp.concatenate([codes_of(key_own), code_two]),
        ]
    )

    def owner(even, odd):
        return jnp.where(core == 0, even(r), odd(r))

    def products(queries, read, one, two):
        rows = [rows_of(queries, row_start(device), 64) for device in (one, two)]
        return partial_of(jnp.concatenate(rows, axis=0), read)

    def blocks(own, pair):
        return jnp.stack([own[:64], pair[:64]]), jnp.stack([own[64:], pair[64:]])

    ahead = [
        owner(lambda q: beside(stride(1)(q)), lambda q: across(triple(1)(q))),
        owner(lambda q: beside(stride(2)(q)), lambda q: across(triple(2)(q))),
    ]
    own_sent = products(payload, keys[0], *ahead)
    own_sent, pair_hidden = lax.optimization_barrier((own_sent, pair_hidden))
    sent = blocks(own_sent, products(pair_hidden, keys[1], *ahead))
    *sent, own, pair = lax.optimization_barrier(sent + (hidden, pair_hidden))
    in_one = line_permute(sent[0], beside, triple(1))
    in_two = line_permute(sent[1], beside, triple(2))
    ends = (owner(stride(1), triple(1)), owner(stride(2), triple(2)))
    one, two = blocks(products(own, keys[0], *ends), products(pair, keys[1], *ends))
    ends = (owner(beside, across), r)
    paired, kept = blocks(products(own, keys[0], *ends), products(pair, keys[1], *ends))
    paired = paired + jnp.where(core == 1, in_one + in_two, 0.0)
    one = one + jnp.where(core == 0, in_one, 0.0)
    two = two + jnp.where(core == 0, in_two, 0.0)
    paired, one, two = lax.optimization_barrier((paired, one, two))
    paired = line_permute(paired, beside, across)
    scores = lax.optimization_barrier(kept + paired)
    one = line_permute(one, stride(1), triple(1))
    two = line_permute(two, stride(2), triple(2))
    scores = (scores + one + two) * score_scale

    usable = jnp.broadcast_to((codes > 0.0)[:, None], scores.shape)
    matches = usable & (codes[:, None] == row_codes[:, :, None])
    total_part = summed_part(scores, usable, vocab)
    pos_part = summed_part(scores, matches, gold)
    stats = jnp.stack([*total_part, *pos_part], axis=1)
    other = core_swap(stats)
    other = jnp.concatenate([other[1:], other[:1]], axis=0)
    total_lse = joined_lse(vocab, total_part, (other[:, 0], other[:, 1]))
    pos_lse = joined_lse(gold, pos_part, (other[:, 2], other[:, 3]))
    spread = jnp.where(usable, jnp.exp(scores - total_lse[..., None]), 0.0) - jnp.where(
        matches, jnp.exp(scores - pos_lse[..., None]), 0.0
    )
    slopes = gathered((weight[..., None] * spread * score_scale).astype(BF), core, r)

    both_hidden = jnp.concatenate([hidden, pair_hidden], axis=0)
    flat = slopes.reshape(2 * SEG, 2 * SEG)
    grad_two = key_grad(flat[:, SEG:], both_hidden).astype(BF)
    grad_two, flat = lax.optimization_barrier((grad_two, flat))
    home_two = dp_permute(grad_two, reverse(key_pairs()))
    pair_one = key_grad(flat[SEG:, :SEG], pair_hidden)
    grad_one = key_grad(flat[:SEG, :SEG], hidden) + jnp.where(core == 1, pair_one, 0.0)
    grad_one, flat = lax.optimization_barrier((grad_one.astype(BF), flat))
    home_one = dp_permute(grad_one, reverse(key_pairs()))
    pair_grad = jnp.dot(flat[SEG:], keys[1], preferred_element_type=F32)
    pair_grad = lax.optimization_barrier(pair_grad) + home_two.astype(F32)
    pair_grad = core_swap(pair_grad.astype(BF))
    own_grad = jnp.dot(flat[:SEG], keys[0], preferred_element_type=F32)
    own_grad = lax.optimization_barrier(own_grad + jnp.where(core == 0, pair_one, 0.0))
    own_grad = lax.optimization_barrier(own_grad + home_one.astype(F32))
    return (own_grad + pair_grad.astype(F32)).astype(BF)


def solution(mesh):
    placed = (P("dp", "tensor"), P("dp"), P("dp"), P("dp"), P("dp"), P("dp"))
    return jax.shard_map(
        per_device, mesh=mesh, in_specs=placed, out_specs=P("dp", "tensor"), check_vma=False
    )
```

```python
import math

import jax
import jax.numpy as jnp
from jax import lax
from jax.sharding import PartitionSpec as P

KW = 3840
SEG = 384
BF = jnp.bfloat16
F32 = jnp.float32


def dp_permute(value, pairs):
    return lax.ppermute(value, "dp", pairs)


def core_swap(value):
    return dp_permute(value, [(i, i ^ 1) for i in range(lax.axis_size("dp"))])


def key_pairs():
    count = lax.axis_size("dp")
    return [(i, (i + (4 if i % 2 == 0 else 2)) % count) for i in range(count)]


def crossed_pairs():
    count = lax.axis_size("dp")
    return [(i, (i + 3) % count) for i in range(count)]


def reverse(pairs):
    return [(target, source) for source, target in pairs]


def triple(steps):
    return lambda r: 3 * (r // 3) + (r + steps) % 3


def stride(steps):
    return lambda r: (r + 2 * steps) % 6


def across(r):
    return (r + 3) % 6


def beside(r):
    return r + 1 - 2 * (r % 2)


def line_permute(value, even_to, odd_to):
    size = lax.axis_size("tensor")
    pairs = [
        (i * size + r, i * size + (odd_to if i % 2 else even_to)(r))
        for i in range(lax.axis_size("dp"))
        for r in range(size)
    ]
    return lax.ppermute(value, ("dp", "tensor"), pairs)


def row_start(device):
    return (device % 3) * 128 + (device // 3) * 64


def rows_of(value, start, size, axis=0):
    return lax.dynamic_slice_in_dim(value, start, size, axis)


def partial_of(queries, keys):
    return lax.dot_general(queries, keys, (((1,), (1,)), ((), ())), preferred_element_type=F32)


def key_grad(slopes, hidden):
    return lax.dot_general(slopes, hidden, (((0,), (0,)), ((), ())), preferred_element_type=F32)


def with_codes(hidden, targets, padding):
    code = jnp.where(padding == 1, targets + 1, 0)
    digits = jnp.stack([code >> 8, code & 255]).astype(BF)
    tail = jnp.pad(digits, ((0, 14), (0, hidden.shape[1] - SEG)))
    return jnp.concatenate([hidden, tail], axis=0)


def codes_of(payload):
    digits = lax.optimization_barrier(payload[SEG:])[:2, :SEG].astype(F32)
    return digits[0] * 256.0 + digits[1]


def summed_part(scores, allowed, outside):
    peak = jnp.maximum(outside, jnp.max(jnp.where(allowed, scores, -1e30), axis=2))
    return peak, jnp.sum(jnp.where(allowed, jnp.exp(scores - peak[..., None]), 0.0), axis=2)


def joined_lse(outside, mine, other):
    peak = jnp.maximum(mine[0], other[0])
    total = mine[1] * jnp.exp(mine[0] - peak) + other[1] * jnp.exp(other[0] - peak)
    return peak + jnp.log(jnp.exp(outside - peak) + total)


def gathered(mine, core, r):
    def owner(even, odd):
        return jnp.where(core == 0, even(r), odd(r))

    paired = line_permute(mine, beside, across)
    one = line_permute(mine, stride(1), triple(1))
    two = line_permute(mine, stride(2), triple(2))
    passed_one = line_permute(jnp.where(core == 0, one, paired), beside, triple(1))
    passed_two = line_permute(jnp.where(core == 0, two, paired), beside, triple(2))
    pieces = (
        (mine, r),
        (paired, owner(beside, across)),
        (one, owner(stride(2), triple(2))),
        (two, owner(stride(1), triple(1))),
        (passed_one, owner(lambda q: beside(stride(2)(q)), lambda q: across(triple(2)(q)))),
        (passed_two, owner(lambda q: beside(stride(1)(q)), lambda q: across(triple(1)(q)))),
    )
    full = jnp.zeros((2, SEG, mine.shape[2]), BF)
    for piece, device in pieces:
        full = lax.dynamic_update_slice_in_dim(full, piece, row_start(device), 1)
    return full


def per_device(hidden, targets, padding, gold_logit, vocab_lse, cotangent):
    score_scale = 1.0 / math.sqrt(KW)
    core = lax.axis_index("dp") % 2
    r = lax.axis_index("tensor")
    payload = lax.optimization_barrier(with_codes(hidden, targets, padding))

    key_one = dp_permute(payload, key_pairs())
    weight = cotangent * padding.astype(F32)
    row_data = jnp.stack([targets.astype(F32) + 1.0, gold_logit, vocab_lse, weight])
    row_data = rows_of(row_data, row_start(r), 64, 1)
    row_data, late_payload = lax.optimization_barrier((row_data, payload))
    key_two = dp_permute(late_payload, crossed_pairs())
    pair_hidden = core_swap(late_payload)[:SEG]
    row_data = jnp.stack([row_data, core_swap(row_data)])
    row_codes, gold, vocab, weight = (row_data[:, i] for i in range(4))

    key_own = jnp.where(core == 0, payload, key_one)
    key_own, key_two = lax.optimization_barrier((key_own, key_two))
    keys = [
        jnp.concatenate([key_one[:SEG], key_two[:SEG]], axis=0),
        jnp.concatenate([key_own[:SEG], key_two[:SEG]], axis=0),
    ]
    code_two = codes_of(key_two)
    codes = jnp.stack(
        [
            jnp.concatenate([codes_of(key_one), code_two]),
            jnp.concatenate([codes_of(key_own), code_two]),
        ]
    )

    def owner(even, odd):
        return jnp.where(core == 0, even(r), odd(r))

    def products(queries, read, one, two):
        rows = [rows_of(queries, row_start(device), 64) for device in (one, two)]
        return partial_of(jnp.concatenate(rows, axis=0), read)

    def blocks(own, pair):
        return jnp.stack([own[:64], pair[:64]]), jnp.stack([own[64:], pair[64:]])

    ahead = [
        owner(lambda q: beside(stride(1)(q)), lambda q: across(triple(1)(q))),
        owner(lambda q: beside(stride(2)(q)), lambda q: across(triple(2)(q))),
    ]
    own_sent = products(payload, keys[0], *ahead)
    own_sent, pair_hidden = lax.optimization_barrier((own_sent, pair_hidden))
    sent = blocks(own_sent, products(pair_hidden, keys[1], *ahead))
    *sent, own, pair = lax.optimization_barrier(sent + (hidden, pair_hidden))
    in_one = line_permute(sent[0], beside, triple(1))
    in_two = line_permute(sent[1], beside, triple(2))
    ends = (owner(stride(1), triple(1)), owner(stride(2), triple(2)))
    one, two = blocks(products(own, keys[0], *ends), products(pair, keys[1], *ends))
    ends = (owner(beside, across), r)
    paired, kept = blocks(products(own, keys[0], *ends), products(pair, keys[1], *ends))
    paired = paired + jnp.where(core == 1, in_one + in_two, 0.0)
    one = one + jnp.where(core == 0, in_one, 0.0)
    two = two + jnp.where(core == 0, in_two, 0.0)
    paired, one, two = lax.optimization_barrier((paired, one, two))
    paired = line_permute(paired, beside, across)
    scores = lax.optimization_barrier(kept + paired)
    one = line_permute(one, stride(1), triple(1))
    two = line_permute(two, stride(2), triple(2))
    scores = (scores + one + two) * score_scale

    usable = jnp.broadcast_to((codes > 0.0)[:, None], scores.shape)
    matches = usable & (codes[:, None] == row_codes[:, :, None])
    total_part = summed_part(scores, usable, vocab)
    pos_part = summed_part(scores, matches, gold)
    stats = jnp.stack([*total_part, *pos_part], axis=1)
    other = core_swap(stats)
    other = jnp.concatenate([other[1:], other[:1]], axis=0)
    total_lse = joined_lse(vocab, total_part, (other[:, 0], other[:, 1]))
    pos_lse = joined_lse(gold, pos_part, (other[:, 2], other[:, 3]))
    spread = jnp.where(usable, jnp.exp(scores - total_lse[..., None]), 0.0) - jnp.where(
        matches, jnp.exp(scores - pos_lse[..., None]), 0.0
    )
    slopes = gathered((weight[..., None] * spread * score_scale).astype(BF), core, r)

    both_hidden = jnp.concatenate([hidden, pair_hidden], axis=0)
    flat = slopes.reshape(2 * SEG, 2 * SEG)
    grad_two = key_grad(flat[:, SEG:], both_hidden).astype(BF)
    grad_two, flat = lax.optimization_barrier((grad_two, flat))
    home_two = dp_permute(grad_two, reverse(key_pairs()))
    pair_one = key_grad(flat[SEG:, :SEG], pair_hidden)
    grad_one = key_grad(flat[:SEG, :SEG], hidden) + jnp.where(core == 1, pair_one, 0.0)
    grad_one, flat = lax.optimization_barrier((grad_one.astype(BF), flat))
    home_one = dp_permute(grad_one, reverse(key_pairs()))
    pair_grad = jnp.dot(flat[SEG:], keys[1], preferred_element_type=F32)
    pair_grad = lax.optimization_barrier(pair_grad) + home_two.astype(F32)
    pair_grad = core_swap(pair_grad.astype(BF))
    own_grad = jnp.dot(flat[:SEG], keys[0], preferred_element_type=F32)
    own_grad = lax.optimization_barrier(own_grad + jnp.where(core == 0, pair_one, 0.0))
    own_grad = lax.optimization_barrier(own_grad + home_one.astype(F32))
    return (own_grad + pair_grad.astype(F32)).astype(BF)


def solution(mesh):
    placed = (P("dp", "tensor"), P("dp"), P("dp"), P("dp"), P("dp"), P("dp"))
    return jax.shard_map(
        per_device, mesh=mesh, in_specs=placed, out_specs=P("dp", "tensor"), check_vma=False
    )
```
